256 devices in a mesh: dp: 32 (over y, x, core), tensor: 8 (over z).
Axes of the slice: x: 4, y: 4, z: 8, core: 2. Of those that a mesh axis runs over, the one named last changes fastest.
Arguments:
- query_rows: bfloat16 [32768, 4096], P('dp', 'tensor'), may hold values from -128 to 128
- key_rows: bfloat16 [32768, 1024], P('dp', 'tensor'), may hold values from -5 to 5
- value_rows: bfloat16 [32768, 1024], P('dp', 'tensor'), may hold values from -6 to 6
- out_grad: bfloat16 [16384, 4096], P('dp', 'tensor'), may hold values from -12 to 12
- w_out: bfloat16 [4096, 4096], P('tensor'), may hold values from -0.09375 to 0.09375
- lengths: int32 [32, 32], replicated, may hold values from 0 to 32, as said below
- target: int32 [32, 32], replicated, may hold values from 0 to 31, as said below
Outputs:
- layer_out: bfloat16 [16384, 4096], P('dp', 'tensor')
- grad_queries: bfloat16 [32768, 4096], P('dp', 'tensor')
- grad_keys: bfloat16 [32768, 1024], P('dp', 'tensor')
- grad_values: bfloat16 [32768, 1024], P('dp', 'tensor')
- weight_grad: float32 [4096, 4096], P('tensor', 'dp')
The draws below stay inside these ranges and needn't reach their ends.
Inputs may be any that keep to these rules, and one draw needn't show every extreme that they name: `lengths`: documents of a replica fill its pack from the first row in the order of j; some document has exactly 32 rows. `target`: each row is a permutation of the replicas. Every replica receives exactly 512 rows in all.
All inputs are finite; a program needn't handle non-finite values.
Results may differ from the reference program's by a relative error of at most 0.022.
Values may be sent and summed in bfloat16 or wider, within the bound.
A program may use at most 128 MiB of HBM per device.

```python
import jax
import jax.numpy as jnp
from jax import lax

D = 4096
QH = 32
KVH = 8
HD = 128
MOST = 32
PACK = 1024
CAP = 512
ROWS = 32768
BALANCED = 16384
N_DP = 32
N_TENSOR = 8


def plan_tables(key):
    sources = N_DP
    half_most = MOST // 2
    base_key = jax.random.fold_in(key, 101)
    pair_key, rank_key, sign_key, row_key, col_key, amount_key, order_key = jax.random.split(base_key, 7)
    lower_half = jax.random.randint(pair_key, (sources // 2,), 0, half_most + 1)
    lower_half = lower_half.at[0].set(half_most)
    offsets = jnp.concatenate([lower_half, -lower_half])[jax.random.permutation(rank_key, sources)]
    signs = jnp.where(jnp.arange(sources) < 3 * sources // 4, 1, -1)[jax.random.permutation(sign_key, sources)]
    load_table = half_most + offsets[:, None] * signs[None, :]
    row_perm = jax.random.permutation(row_key, sources)
    col_perm = jax.random.permutation(col_key, sources)
    row_first = row_perm[0::2]
    row_second = row_perm[1::2]
    col_first = col_perm[0::2]
    col_second = col_perm[1::2]
    headroom = half_most - jnp.maximum(jnp.abs(offsets[row_first]), jnp.abs(offsets[row_second]))
    amounts = jax.random.randint(amount_key, (sources // 2,), 0, headroom + 1)
    load_table = load_table.at[row_first, col_first].add(amounts)
    load_table = load_table.at[row_second, col_second].add(amounts)
    load_table = load_table.at[row_first, col_second].add(-amounts)
    load_table = load_table.at[row_second, col_first].add(-amounts)
    orders = jax.vmap(lambda one_key: jax.random.permutation(one_key, sources))(jax.random.split(order_key, sources))
    lengths = jnp.take_along_axis(load_table, orders, axis=1)
    return (lengths.astype(jnp.int32), orders.astype(jnp.int32))


def key_field(key):
    field_key = jax.random.fold_in(key, 202)
    return jnp.clip(jax.random.normal(field_key, (N_DP * PACK, KVH * HD), jnp.float32), -4.0, 4.0)


def draw_lengths(key, part):
    lengths, orders = plan_tables(key)
    return lengths


def draw_target(key, part):
    lengths, orders = plan_tables(key)
    return orders


def draw_key_rows(key, part):
    field_rows = key_field(key)
    return field_rows.astype(jnp.bfloat16)


def draw_query_rows(key, part):
    key = jax.random.fold_in(key, 3)
    normal_key = jax.random.fold_in(key, 0)
    drawn_rows = jax.random.normal(normal_key, (N_DP * PACK, QH * HD), jnp.float32)
    result_rows = jnp.clip(drawn_rows, -4.0, 4.0)
    return result_rows.astype(jnp.bfloat16)


def spiked(values, rng, source, target, blocks, factor):
    def block_of(dim):
        return (jnp.arange(values.shape[dim]) // (values.shape[dim] // blocks)).reshape((-1,) + (1,) * (values.ndim - 1 - dim))

    first = jax.random.permutation(rng, blocks)[block_of(target)]
    other_side = (block_of(target) + blocks // 2) % blocks
    return jnp.where((block_of(source) == first) | (block_of(source) == other_side), factor * values, values)


def level_of(stream_key, shape, cuts, least, top_value):
    factor_of = 1.0
    for dim, parts in cuts:
        draws = jax.random.uniform(jax.random.fold_in(jax.random.fold_in(stream_key, 6), dim), (parts,), jnp.float32, least / len(cuts), top_value / len(cuts))
        factor_of = factor_of * jnp.repeat(jnp.exp(draws), shape[dim] // parts).reshape((-1,) + (1,) * (len(shape) - 1 - dim))
    return factor_of


def gaussian(own_key, extent, width, reach, cuts=(), kind=jnp.bfloat16):
    values = jax.random.normal(own_key, extent, jnp.float32) * width
    if len(cuts) > 0:
        values = level_of(own_key, extent, cuts, -0.22, 0.18) * values
    return jnp.clip(values, min=-reach, max=reach).astype(kind)


def gaussian_with(stream_key, shape, width, most, shards, heavy, held_as=jnp.bfloat16):
    drawn = width * jax.random.normal(stream_key, shape, jnp.float32)
    if shards:
        drawn = drawn * level_of(stream_key, shape, shards, -0.22, 0.18)
    return jnp.clip(spiked(drawn, jax.random.fold_in(stream_key, 3), *heavy), -most, most).astype(held_as)


def setup_inputs(seed: int = 0) -> dict:
    keys = jax.random.split(jax.random.key(seed), 8)
    query_rows = draw_query_rows(jax.random.fold_in(keys[7], 71), 0)
    key_rows = draw_key_rows(jax.random.fold_in(keys[7], 71), 0)
    value_rows = gaussian(keys[2], (ROWS, KVH * HD), 1.0, 6.0, ((0, 32), (1, 8)))
    out_grad = gaussian_with(keys[3], (BALANCED, D), 1.0, 12.0, ((0, 32), (1, 8)), (0, 1, 32, 2.75))
    w_out = gaussian(keys[4], (QH * HD, D), (QH * HD) ** -0.5, 0.09375, ((0, 8),))
    lengths = draw_lengths(jax.random.fold_in(keys[7], 71), 0)
    target = draw_target(jax.random.fold_in(keys[7], 71), 0)
    return dict(query_rows=query_rows, key_rows=key_rows, value_rows=value_rows, out_grad=out_grad, w_out=w_out, lengths=lengths, target=target)


neg_large = -1e30


def doc_tables(lengths, target):
    sources = lengths.shape[0]
    doc_ends = jnp.cumsum(lengths, axis=1).astype(jnp.int32)
    doc_starts = (doc_ends - lengths).astype(jnp.int32)
    replica_ids = jnp.arange(sources, dtype=jnp.int32)
    matches = (target[:, :, None] == replica_ids[None, None, :]).astype(jnp.int32)
    start_table = jnp.sum(matches * doc_starts[:, :, None], axis=1).astype(jnp.int32)
    length_table = jnp.sum(matches * lengths[:, :, None], axis=1).astype(jnp.int32)
    return start_table, length_table


def allowed_mask(piece_len, piece_rows):
    slot_ids = jnp.arange(piece_rows, dtype=jnp.int32)
    causal = slot_ids[None, :] <= slot_ids[:, None]
    inside = slot_ids[None, None, :] < piece_len[:, None, None]
    diagonal = slot_ids[None, :] == slot_ids[:, None]
    return (causal[None] & inside) | diagonal[None]


def split_heads(query_pieces, key_pieces):
    sources, piece_rows, query_cols = query_pieces.shape
    kv_heads = key_pieces.shape[2] // HD
    group_size = query_cols // HD // kv_heads
    return sources, piece_rows, query_cols, kv_heads, group_size


def piece_forward(query_pieces, key_pieces, value_pieces, piece_len):
    sources, piece_rows, query_cols, kv_heads, group_size = split_heads(query_pieces, key_pieces)
    query_heads = query_pieces.reshape(sources, piece_rows, kv_heads, group_size, HD).astype(jnp.float32)
    key_heads = key_pieces.reshape(sources, piece_rows, kv_heads, HD).astype(jnp.float32)
    value_heads = value_pieces.reshape(sources, piece_rows, kv_heads, HD).astype(jnp.float32)
    scores = jnp.einsum("bqcgh,bkch->bcgqk", query_heads, key_heads) * (HD ** -0.5)
    allowed = allowed_mask(piece_len, piece_rows)
    scores = jnp.where(allowed[:, None, None], scores, neg_large)
    row_max = jnp.max(scores, axis=-1, keepdims=True)
    weights = jnp.exp(scores - row_max)
    weights = weights / jnp.sum(weights, axis=-1, keepdims=True)
    weights_half = weights.astype(jnp.bfloat16).astype(jnp.float32)
    context = jnp.einsum("bcgqk,bkch->bqcgh", weights_half, value_heads)
    return context.astype(jnp.bfloat16).reshape(sources, piece_rows, query_cols), weights


def piece_backward(query_pieces, key_pieces, value_pieces, context, dcontext, weights):
    sources, piece_rows, query_cols, kv_heads, group_size = split_heads(query_pieces, key_pieces)
    query_heads = query_pieces.reshape(sources, piece_rows, kv_heads, group_size, HD).astype(jnp.float32)
    key_heads = key_pieces.reshape(sources, piece_rows, kv_heads, HD).astype(jnp.float32)
    value_heads = value_pieces.reshape(sources, piece_rows, kv_heads, HD).astype(jnp.float32)
    context_heads = context.reshape(sources, piece_rows, kv_heads, group_size, HD).astype(jnp.float32)
    dcontext_heads = dcontext.reshape(sources, piece_rows, kv_heads, group_size, HD).astype(jnp.float32)
    weights_half = weights.astype(jnp.bfloat16).astype(jnp.float32)
    dvalues = jnp.einsum("bcgqk,bqcgh->bkch", weights_half, dcontext_heads)
    dweights = jnp.einsum("bqcgh,bkch->bcgqk", dcontext_heads, value_heads)
    row_delta = jnp.sum(dcontext_heads * context_heads, axis=-1)
    row_delta = jnp.transpose(row_delta, (0, 2, 3, 1))[..., None]
    dscores = (weights * (dweights - row_delta) * (HD ** -0.5)).astype(jnp.bfloat16).astype(jnp.float32)
    dqueries = jnp.einsum("bcgqk,bkch->bqcgh", dscores, key_heads)
    dkeys = jnp.einsum("bcgqk,bqcgh->bkch", dscores, query_heads)
    return (dqueries.astype(jnp.bfloat16).reshape(sources, piece_rows, query_cols),
            dkeys.astype(jnp.bfloat16).reshape(sources, piece_rows, kv_heads * HD),
            dvalues.astype(jnp.bfloat16).reshape(sources, piece_rows, kv_heads * HD))


def reference(query_rows, key_rows, value_rows, out_grad, w_out, lengths, target):
    sources = N_DP
    piece_rows = MOST
    home_rows = N_DP * PACK
    balanced_rows = N_DP * CAP
    start_table, length_table = doc_tables(lengths, target)
    slot_ids = jnp.arange(piece_rows, dtype=jnp.int32)
    replica_ids = jnp.arange(sources, dtype=jnp.int32)
    is_live = slot_ids[None, None, :] < length_table[:, :, None]
    home_index = replica_ids[:, None, None] * PACK + start_table[:, :, None] + slot_ids[None, None, :]
    home_index = jnp.where(is_live, home_index, home_rows).astype(jnp.int32).reshape(-1)
    live_flat = is_live.reshape(-1)

    def pieces_of(array):
        gathered = jnp.take(array, jnp.minimum(home_index, home_rows - 1).astype(jnp.int32), axis=0)
        gathered = jnp.where(live_flat[:, None], gathered, jnp.zeros_like(gathered))
        return gathered.reshape(sources * sources, piece_rows, array.shape[1])

    query_pieces = pieces_of(query_rows)
    key_pieces = pieces_of(key_rows)
    value_pieces = pieces_of(value_rows)
    piece_len = length_table.reshape(-1)
    context, weights = piece_forward(query_pieces, key_pieces, value_pieces, piece_len)

    col_starts = (jnp.cumsum(length_table, axis=0) - length_table).astype(jnp.int32)
    balanced_index = replica_ids[None, :, None] * CAP + col_starts[:, :, None] + slot_ids[None, None, :]
    balanced_index = jnp.where(is_live, balanced_index, balanced_rows).astype(jnp.int32).reshape(-1)
    flat_context = context.reshape(-1, context.shape[2])
    balanced_context = jnp.zeros((balanced_rows, flat_context.shape[1]), jnp.bfloat16)
    balanced_context = balanced_context.at[balanced_index].set(flat_context, mode="drop")

    shard_cols = QH * HD // N_TENSOR
    running = jnp.zeros((balanced_rows, D), jnp.float32)
    for shard_id in range(N_TENSOR):
        low_col = shard_id * shard_cols
        partial_value = jnp.dot(balanced_context[:, low_col:low_col + shard_cols], w_out[low_col:low_col + shard_cols],
                          preferred_element_type=jnp.float32)
        rounded = lax.optimization_barrier(partial_value.astype(jnp.bfloat16))
        running = running + rounded.astype(jnp.float32)
    layer_out = running.astype(jnp.bfloat16)

    dbalanced = jnp.dot(out_grad, w_out.T, preferred_element_type=jnp.float32).astype(jnp.bfloat16)
    weight_grad = jnp.dot(balanced_context.T, out_grad, preferred_element_type=jnp.float32)
    dcontext = jnp.take(dbalanced, jnp.minimum(balanced_index, balanced_rows - 1).astype(jnp.int32), axis=0)
    dcontext = jnp.where(live_flat[:, None], dcontext, jnp.zeros_like(dcontext))
    dcontext = dcontext.reshape(sources * sources, piece_rows, -1)
    dquery_pieces, dkey_pieces, dvalue_pieces = piece_backward(query_pieces, key_pieces, value_pieces,
                                                               context, dcontext, weights)

    def rows_of(pieces):
        flat_rows = pieces.reshape(-1, pieces.shape[2])
        output = jnp.zeros((home_rows, flat_rows.shape[1]), flat_rows.dtype)
        return output.at[home_index].set(flat_rows, mode="drop")

    return layer_out, rows_of(dquery_pieces), rows_of(dkey_pieces), rows_of(dvalue_pieces), weight_grad
```

```python
import jax
import jax.numpy as jnp
from jax import lax
from jax.sharding import PartitionSpec as P

HD = 128


neg_large = -1e30


def doc_tables(lengths, target):
    sources = lengths.shape[0]
    doc_ends = jnp.cumsum(lengths, axis=1)
    doc_starts = doc_ends - lengths
    replica_ids = jnp.arange(sources, dtype=jnp.int32)
    matches = (target[:, :, None] == replica_ids[None, None, :]).astype(jnp.int32)
    start_table = jnp.sum(matches * doc_starts[:, :, None], axis=1)
    length_table = jnp.sum(matches * lengths[:, :, None], axis=1)
    return (start_table, length_table)


def home_layout(start_row, length_row, piece_rows, home_rows):
    slot_ids = jnp.arange(piece_rows, dtype=jnp.int32)
    row_index = start_row[:, None] + slot_ids[None, :]
    is_live = slot_ids[None, :] < length_row[:, None]
    row_index = jnp.where(is_live, row_index, home_rows).reshape(-1)
    return (row_index, is_live.reshape(-1))


def balanced_layout(length_col, piece_rows, balanced_rows):
    sources = length_col.shape[0]
    col_ends = jnp.cumsum(length_col)
    col_starts = col_ends - length_col
    row_ids = jnp.arange(balanced_rows, dtype=jnp.int32)
    source_of = jnp.sum((row_ids[:, None] >= col_ends[None, :]).astype(jnp.int32), axis=1)
    matches = (source_of[:, None] == jnp.arange(sources, dtype=jnp.int32)[None, :]).astype(
        jnp.int32
    )
    begin_of = jnp.sum(matches * col_starts[None, :], axis=1)
    return source_of * piece_rows + row_ids - begin_of


def to_pieces(array, row_index, is_live, piece_rows):
    last_row = array.shape[0] - 1
    gathered = jnp.take(array, jnp.minimum(row_index, last_row), axis=0)
    gathered = jnp.where(is_live[:, None], gathered, jnp.zeros_like(gathered))
    return gathered.reshape(-1, piece_rows, array.shape[1])


def from_pieces(pieces, row_index, home_rows):
    flat_rows = pieces.reshape(-1, pieces.shape[2])
    output = jnp.zeros((home_rows, flat_rows.shape[1]), flat_rows.dtype)
    return output.at[row_index].set(flat_rows, mode="drop")


def allowed_mask(piece_len, piece_rows):
    slot_ids = jnp.arange(piece_rows, dtype=jnp.int32)
    causal = slot_ids[None, :] <= slot_ids[:, None]
    inside = slot_ids[None, None, :] < piece_len[:, None, None]
    diagonal = slot_ids[None, :] == slot_ids[:, None]
    return causal[None] & inside | diagonal[None]


def split_heads(query_pieces, key_pieces):
    sources, piece_rows, query_cols = query_pieces.shape
    kv_heads = key_pieces.shape[2] // HD
    group_size = query_cols // HD // kv_heads
    return (sources, piece_rows, query_cols, kv_heads, group_size)


def piece_forward(query_pieces, key_pieces, value_pieces, piece_len):
    sources, piece_rows, query_cols, kv_heads, group_size = split_heads(query_pieces, key_pieces)
    query_heads = query_pieces.reshape(sources, piece_rows, kv_heads, group_size, HD)
    key_heads = key_pieces.reshape(sources, piece_rows, kv_heads, HD)
    value_heads = value_pieces.reshape(sources, piece_rows, kv_heads, HD)
    scores = jnp.einsum(
        "bqcgh,bkch->bcgqk", query_heads, key_heads, preferred_element_type=jnp.float32
    ) * HD ** (-0.5)
    allowed = allowed_mask(piece_len, piece_rows)
    scores = jnp.where(allowed[:, None, None], scores, neg_large)
    row_max = jnp.max(scores, axis=-1, keepdims=True)
    weights = jnp.exp(scores - row_max)
    weights = weights / jnp.sum(weights, axis=-1, keepdims=True)
    context = jnp.einsum(
        "bcgqk,bkch->bqcgh",
        weights.astype(jnp.bfloat16),
        value_heads,
        preferred_element_type=jnp.float32,
    )
    return (context.astype(jnp.bfloat16).reshape(sources, piece_rows, query_cols), weights)


def piece_backward(query_pieces, key_pieces, value_pieces, context, dcontext, weights):
    sources, piece_rows, query_cols, kv_heads, group_size = split_heads(query_pieces, key_pieces)
    query_heads = query_pieces.reshape(sources, piece_rows, kv_heads, group_size, HD)
    key_heads = key_pieces.reshape(sources, piece_rows, kv_heads, HD)
    value_heads = value_pieces.reshape(sources, piece_rows, kv_heads, HD)
    context_heads = context.reshape(sources, piece_rows, kv_heads, group_size, HD)
    dcontext_heads = dcontext.reshape(sources, piece_rows, kv_heads, group_size, HD)
    dvalues = jnp.einsum(
        "bcgqk,bqcgh->bkch",
        weights.astype(jnp.bfloat16),
        dcontext_heads,
        preferred_element_type=jnp.float32,
    )
    dweights = jnp.einsum(
        "bqcgh,bkch->bcgqk", dcontext_heads, value_heads, preferred_element_type=jnp.float32
    )
    row_delta = jnp.sum(
        dcontext_heads.astype(jnp.float32) * context_heads.astype(jnp.float32), axis=-1
    )
    row_delta = jnp.transpose(row_delta, (0, 2, 3, 1))[..., None]
    dscores = (weights * (dweights - row_delta) * HD ** (-0.5)).astype(jnp.bfloat16)
    dqueries = jnp.einsum(
        "bcgqk,bkch->bqcgh", dscores, key_heads, preferred_element_type=jnp.float32
    )
    dkeys = jnp.einsum(
        "bcgqk,bqcgh->bkch", dscores, query_heads, preferred_element_type=jnp.float32
    )
    return (
        dqueries.astype(jnp.bfloat16).reshape(sources, piece_rows, query_cols),
        dkeys.astype(jnp.bfloat16).reshape(sources, piece_rows, kv_heads * HD),
        dvalues.astype(jnp.bfloat16).reshape(sources, piece_rows, kv_heads * HD),
    )


def fold_factory(context_rows, w_out, block_in):
    dcontext = lax.dot_general(
        block_in, w_out, (((1,), (1,)), ((), ())), preferred_element_type=jnp.float32
    )
    block_grad = lax.dot_general(
        context_rows, block_in, (((0,), (0,)), ((), ())), preferred_element_type=jnp.float32
    )
    return (dcontext, block_grad)


def shards(query_rows, key_rows, value_rows, out_grad, w_out, lengths, target):
    home_rows = query_rows.shape[0]
    balanced_rows = out_grad.shape[0]
    sources = lengths.shape[0]
    piece_rows = home_rows // sources
    query_cols = w_out.shape[0]
    own_index = lax.axis_index("dp")
    grad_rows = lax.all_gather(out_grad, "tensor", axis=1, tiled=True)
    start_table, length_table = doc_tables(lengths, target)
    start_row = lax.dynamic_index_in_dim(start_table, own_index, 0, keepdims=False)
    length_row = lax.dynamic_index_in_dim(length_table, own_index, 0, keepdims=False)
    length_col = lax.dynamic_index_in_dim(length_table, own_index, 1, keepdims=False)
    row_index, is_live = home_layout(start_row, length_row, piece_rows, home_rows)
    balanced_index = balanced_layout(length_col, piece_rows, balanced_rows)
    query_pieces = to_pieces(query_rows, row_index, is_live, piece_rows)
    key_pieces = to_pieces(key_rows, row_index, is_live, piece_rows)
    value_pieces = to_pieces(value_rows, row_index, is_live, piece_rows)
    context, weights = piece_forward(query_pieces, key_pieces, value_pieces, length_row)
    arrived = lax.all_to_all(context, "dp", split_axis=0, concat_axis=0, tiled=True)
    balanced_context = jnp.take(arrived.reshape(home_rows, query_cols), balanced_index, axis=0)
    partial_value = jnp.dot(balanced_context, w_out, preferred_element_type=jnp.float32)
    layer_out = lax.psum_scatter(
        partial_value.astype(jnp.bfloat16), "tensor", scatter_dimension=1, tiled=True
    )
    dbalanced, weight_part = fold_factory(balanced_context, w_out, grad_rows)
    spread = (
        jnp.zeros((home_rows, query_cols), jnp.bfloat16)
        .at[balanced_index]
        .set(dbalanced.astype(jnp.bfloat16))
    )
    dcontext = lax.all_to_all(
        spread.reshape(sources, piece_rows, query_cols),
        "dp",
        split_axis=0,
        concat_axis=0,
        tiled=True,
    )
    dquery_pieces, dkey_pieces, dvalue_pieces = piece_backward(
        query_pieces, key_pieces, value_pieces, context, dcontext, weights
    )
    grad_queries = from_pieces(dquery_pieces, row_index, home_rows)
    grad_keys = from_pieces(dkey_pieces, row_index, home_rows)
    grad_values = from_pieces(dvalue_pieces, row_index, home_rows)
    weight_grad = lax.psum_scatter(
        weight_part.astype(jnp.bfloat16), "dp", scatter_dimension=1, tiled=True
    ).astype(jnp.float32)
    return (layer_out, grad_queries, grad_keys, grad_values, weight_grad)


def solution(mesh):
    return jax.shard_map(
        shards,
        mesh=mesh,
        in_specs=(
            P("dp", "tensor"),
            P("dp", "tensor"),
            P("dp", "tensor"),
            P("dp", "tensor"),
            P("tensor", None),
            P(),
            P(),
        ),
        out_specs=(
            P("dp", "tensor"),
            P("dp", "tensor"),
            P("dp", "tensor"),
            P("dp", "tensor"),
            P("tensor", "dp"),
        ),
        check_vma=False,
    )
```

```python
import jax
import jax.numpy as jnp
from jax import lax
from jax.experimental import pallas as pl
from jax.experimental.pallas import tpu as pltpu
from jax.sharding import PartitionSpec as P

HD = 128
GROUP = 4
QC = GROUP * HD
XC = QC + 2 * HD
SLOT = 32
NDP = 32
NCHIP = NDP // 2
NT = 8
PACK = NDP * SLOT
CAP = 512
MC = 512
TILE = 128
HALF = CAP // 2
SCALE = HD**-0.5
OFF = 4096.0
BF = jnp.bfloat16
F32 = jnp.float32
MESH = pl.DeviceIdType.MESH


def nn(a, b):
    return lax.dot_general(a, b, (((1,), (0,)), ((), ())), preferred_element_type=F32)


def nt(a, b):
    return lax.dot_general(a, b, (((1,), (1,)), ((), ())), preferred_element_type=F32)


def tn(a, b):
    return lax.dot_general(a, b, (((0,), (0,)), ((), ())), preferred_element_type=F32)


def iota(shape, dim):
    return lax.broadcasted_iota(jnp.int32, shape, dim)


def one_hot(mask):
    return jnp.where(mask, 1.0, 0.0).astype(BF)


def remote(src, dst, send, recv, where):
    return pltpu.make_async_remote_copy(
        src_ref=src, dst_ref=dst, send_sem=send, recv_sem=recv, device_id=where, device_id_type=MESH
    )


def slot_index(member, starts, sizes):
    high = jnp.floor(starts * (1.0 / SLOT))
    low = starts - high * SLOT
    slot_col = (iota((PACK, 1), 0) % SLOT).astype(F32)
    slot_row = (iota((1, PACK), 1) % SLOT).astype(F32)
    start_col = jnp.sum(jnp.where(member, starts[0:1], 0.0), axis=1, keepdims=True)
    size_col = jnp.sum(jnp.where(member, sizes[0:1], 0.0), axis=1, keepdims=True)
    picks = one_hot(member)
    start_row = nt(high.astype(BF), picks)[0:1] * SLOT + nt(low.astype(BF), picks)[0:1]
    size_row = nt(sizes.astype(BF), picks)[0:1]
    col = jnp.where(slot_col < size_col, start_col + slot_col, OFF)
    row = jnp.where(slot_row < size_row, start_row + slot_row, OFF)
    return col, row


def kernel(
    q_in, k_in, v_in, og_in, w_in, len_ref, tgt_ref,
    lo_ref, gq_ref, gk_ref, gv_ref, wg_ref,
    home, pieces, og, w, perm, perm_t, sel, sel_t, home_col, home_row, bal_col, bal_row, bias, probs,
    ctx_send, ctx_recv, bctx, bctx_t, part, rs_recv, dbal, wp, sx, wr, d_send, d_recv, gp,
    load_sem, ag_send, ag_recv, rs_send, rs_recv_sem, c_send, c_recv, d_ssem, d_rsem,
    x_send, x_recv, w_send, w_recv,
):
    me = lax.axis_index("dp")
    z = lax.axis_index("tensor")
    core = lax.rem(me, 2)
    chip = lax.div(me, 2)
    right, left = {"tensor": lax.rem(z + 1, NT)}, {"tensor": lax.rem(z + NT - 1, NT)}
    toward = (right, left)
    sibling = {"dp": me + 1 - 2 * core}

    loads = [
        pltpu.make_async_copy(q_in, home.at[:, pl.ds(0, QC)], load_sem.at[0]),
        pltpu.make_async_copy(k_in, home.at[:, pl.ds(QC, HD)], load_sem.at[1]),
        pltpu.make_async_copy(v_in, home.at[:, pl.ds(QC + HD, HD)], load_sem.at[2]),
        pltpu.make_async_copy(og_in, og.at[0], load_sem.at[3]),
        pltpu.make_async_copy(w_in, w, load_sem.at[4]),
    ]
    for one in (loads[3], loads[0], loads[1], loads[2], loads[4]):
        one.start()

    barrier = pltpu.get_barrier_semaphore()
    pl.semaphore_signal(barrier, inc=1, device_id=right, device_id_type=MESH)
    pl.semaphore_signal(barrier, inc=1, device_id=left, device_id_type=MESH)

    @pl.loop(1, NDP)
    def _(k):
        pl.semaphore_signal(
            barrier, inc=1, device_id={"dp": lax.rem(me + k, NDP)}, device_id_type=MESH
        )

    pl.semaphore_wait(barrier, NDP + 1)

    halves = (pl.ds(0, HALF), pl.ds(HALF, HALF))

    def ag_copy(way, step, half):
        src = (NT - step) % NT if way == 0 else step
        dst = (NT - step - 1) % NT if way == 0 else step + 1
        return remote(
            og.at[src, halves[half]],
            og.at[dst, halves[half]],
            ag_send.at[way, step, half],
            ag_recv.at[way, step, half],
            toward[way],
        )

    def ag_halves(way, step):
        return (0, 1) if step < 3 else (way,)

    def ag_step(step):
        for half in (0, 1):
            for way in (0, 1):
                if step > 0:
                    ag_copy(way, step - 1, half if way == 0 else 1 - half).wait_recv()
                order = half if way == 0 else 1 - half
                if order in ag_halves(way, step):
                    ag_copy(way, step, order).start()

    loads[3].wait()
    ag_step(0)

    lane = iota((NDP, NDP), 1)
    before = jnp.where(iota((NDP, NDP), 0) < lane, 1.0, 0.0).astype(BF)
    sizes = jnp.broadcast_to(len_ref[pl.ds(me, 1), :].astype(F32), (8, NDP))
    starts = nn(sizes.astype(BF), before)
    doc_of = lax.div(iota((PACK, NDP), 0), SLOT)
    col, row = slot_index(tgt_ref[pl.ds(me, 1), :] == doc_of, starts, sizes)
    home_col[...] = jnp.broadcast_to(col, (PACK, 128))
    home_row[...] = jnp.broadcast_to(row, (8, PACK))

    @pl.loop(0, PACK // TILE)
    def _(i):
        rows = pl.ds(pl.multiple_of(i * TILE, TILE), TILE)
        index = home_col[rows, 0:1]
        perm[rows, :] = one_hot(index == iota((TILE, PACK), 1).astype(F32))

    for one in loads[:3]:
        one.wait()

    @pl.loop(0, XC // 256)
    def _(i):
        cols = pl.ds(pl.multiple_of(i * 256, 256), 256)
        pieces[:, cols] = nn(perm[...], home[:, cols]).astype(BF)

    key_row = iota((TILE, QC), 0)
    query_row = iota((TILE, QC), 1) % TILE
    allowed = (lax.div(key_row, SLOT) == lax.div(query_row, SLOT)) & (key_row <= query_row)
    bias[...] = jnp.where(allowed, 0.0, -1e30)

    def heads(ref, rows):
        return jnp.concatenate([ref[rows, h * HD : (h + 1) * HD] for h in range(GROUP)], axis=0)

    @pl.loop(0, PACK // TILE)
    def _(i):
        rows = pl.ds(pl.multiple_of(i * TILE, TILE), TILE)
        scores = nt(pieces[rows, QC : QC + HD], heads(pieces, rows)) * SCALE + bias[...]
        weights = jnp.exp(scores - jnp.max(scores, axis=0, keepdims=True))
        weights = weights / jnp.sum(weights, axis=0, keepdims=True)
        probs[i] = weights
        context = tn(weights.astype(BF), pieces[rows, QC + HD : XC]).astype(BF)
        for h in range(GROUP):
            ctx_send[rows, h * HD : (h + 1) * HD] = context[h * TILE : (h + 1) * TILE]

    def piece(d):
        return pl.ds(pl.multiple_of(d * SLOT, SLOT), SLOT)

    def exchange_start(source, dest, send, recv):
        @pl.loop(1, NDP)
        def _(k):
            d = lax.rem(me + k, NDP)
            remote(
                source.at[piece(d)], dest.at[piece(me)], send.at[d], recv.at[me], {"dp": d}
            ).start()

        dest[piece(me), :] = source[piece(me), :]

    def exchange_wait(source, dest, send, recv):
        @pl.loop(1, NDP)
        def _(k):
            d = lax.rem(me + k, NDP)
            remote(
                source.at[piece(d)], dest.at[piece(d)], send.at[d], recv.at[d], {"dp": d}
            ).wait()

    exchange_start(ctx_send, ctx_recv, c_send, c_recv)

    sent_here = jnp.where(tgt_ref[...] == me, len_ref[...], 0).astype(F32).astype(BF)
    sizes = nt(jnp.ones((8, NDP), BF), sent_here)
    starts = nn(sizes.astype(BF), before)
    col, row = slot_index(iota((PACK, NDP), 1) == doc_of, starts, sizes)
    bal_col[...] = jnp.broadcast_to(col, (PACK, 128))
    bal_row[...] = jnp.broadcast_to(row, (8, PACK))

    @pl.loop(0, CAP // TILE)
    def _(i):
        rows = pl.ds(pl.multiple_of(i * TILE, TILE), TILE)
        here = (iota((TILE, PACK), 0) + i * TILE).astype(F32)
        sel[rows, :] = one_hot(bal_row[0:1, :] == here)

    loads[4].wait()
    ag_step(1)

    def model_cols(rel):
        owner = lax.rem(z + rel, NT)
        return owner, pl.ds(pl.multiple_of(owner * MC, MC), MC)

    def add_dbalanced(rel, first=False):
        _, cols = model_cols(rel)
        term = nt(og[rel], w[:, cols])
        dbal[...] = term if first else dbal[...] + term

    add_dbalanced(0, True)
    add_dbalanced(1)
    add_dbalanced(7)

    @pl.loop(0, PACK // TILE)
    def _(i):
        rows = pl.ds(pl.multiple_of(i * TILE, TILE), TILE)
        here = (iota((TILE, PACK), 0) + i * TILE).astype(F32)
        perm_t[rows, :] = one_hot(home_row[0:1, :] == here)
        index = bal_col[rows, 0:1]
        sel_t[rows, :] = one_hot(index == iota((TILE, CAP), 1).astype(F32))

    ag_step(2)
    add_dbalanced(2)
    add_dbalanced(6)

    exchange_wait(ctx_send, ctx_recv, c_send, c_recv)
    balanced = nn(sel[...], ctx_recv[...]).astype(BF)
    bctx[...] = balanced
    bctx_t[...] = balanced.T

    def project(rel):
        _, cols = model_cols(rel)
        part[rel] = nn(bctx[...], w[:, cols]).astype(BF)

    def rs_copy(way, step, half):
        rel = 4 - step if way == 0 else 4 + step
        return remote(
            part.at[rel, halves[half]],
            rs_recv.at[way, step, halves[half]],
            rs_send.at[way, step, half],
            rs_recv_sem.at[way, step, half],
            toward[way],
        )

    def rs_step(step, late=False):
        for half in (0, 1):
            for way in (0, 1):
                order = half if way == 0 else 1 - half
                rel = 4 - step if way == 0 else 4 + step
                if order in ag_halves(way, 3 if step == 1 else 0):
                    rs_copy(way, step - 1, order).wait_recv()
                    rows = halves[order]
                    total = part[rel, rows].astype(F32) + rs_recv[way, step - 1, rows].astype(F32)
                    part[rel, rows] = total.astype(BF)
                    rs_copy(way, step, order).start()

    def weight_block(rel):
        owner, _ = model_cols(rel)
        grad = nn(bctx_t[...], og[rel]).astype(BF)
        for j in range(4):
            wp[lax.rem(core + j, 2), 2 * owner + j // 2] = grad[:, j * 128 : (j + 1) * 128]

    def sibling_copy(rel):
        owner, _ = model_cols(rel)
        both = pl.ds(2 * owner, 2)
        return remote(wp.at[1, both], sx.at[both], x_send.at[rel], x_recv.at[rel], sibling)

    def weight_copy(m, slot):
        return remote(
            wp.at[0, m], wr.at[slot], w_send.at[m], w_recv.at[slot], {"dp": 2 * m + core}
        )

    def weight_send(rel):
        owner, _ = model_cols(rel)
        sibling_copy(rel).wait_recv()
        for j in range(2):
            m = 2 * owner + j
            total = (wp[0, m].astype(F32) + sx[m].astype(F32)).astype(BF)
            wp[0, m] = total

            @pl.when(m != chip)
            def _():
                weight_copy(m, chip).start()

            @pl.when(m == chip)
            def _():
                wr[m] = total

    project(4)
    rs_copy(0, 0, 0).start()
    rs_copy(1, 0, 1).start()
    for rel in (0, 1, 7):
        weight_block(rel)
        sibling_copy(rel).start()
    ag_step(3)
    project(3)
    project(5)
    add_dbalanced(3)
    add_dbalanced(5)
    for rel in (2, 6):
        weight_block(rel)
        sibling_copy(rel).start()
    for rel in (0, 1, 7):
        weight_send(rel)
    ag_copy(0, 3, 0).wait_recv()
    ag_copy(1, 3, 1).wait_recv()
    rs_copy(0, 1, 1).start()
    rs_copy(1, 1, 0).start()
    add_dbalanced(4)
    d_send[...] = nn(sel_t[...], dbal[...].astype(BF)).astype(BF)
    exchange_start(d_send, d_recv, d_ssem, d_rsem)
    rs_step(1)
    for rel in (3, 5, 4):
        weight_block(rel)
        sibling_copy(rel).start()
    project(2)
    project(6)
    for rel in (2, 6):
        weight_send(rel)
    rs_step(2)
    project(1)
    project(7)
    for rel in (3, 5, 4):
        weight_send(rel)
    project(0)
    exchange_wait(d_send, d_recv, d_ssem, d_rsem)

    def backward(low, high):
        @pl.loop(low, high)
        def _(i):
            rows = pl.ds(pl.multiple_of(i * TILE, TILE), TILE)
            weights = probs[i]
            half = weights.astype(BF)
            dcontext = heads(d_recv, rows)
            dweights = nt(pieces[rows, QC + HD : XC], dcontext)
            delta = jnp.sum(half.astype(F32) * dweights, axis=0, keepdims=True)
            dscores = (weights * (dweights - delta) * SCALE).astype(BF)
            dq = tn(dscores, pieces[rows, QC : QC + HD]).astype(BF)
            for h in range(GROUP):
                gp[rows, h * HD : (h + 1) * HD] = dq[h * TILE : (h + 1) * TILE]
            gp[rows, QC : QC + HD] = nn(dscores, heads(pieces, rows)).astype(BF)
            gp[rows, QC + HD : XC] = nn(half, dcontext).astype(BF)

    backward(0, 4)
    rs_step(3)
    backward(4, 8)

    @pl.loop(0, QC // 256)
    def _(i):
        cols = pl.ds(pl.multiple_of(i * 256, 256), 256)
        gq_ref[:, cols] = nn(perm_t[...], gp[:, cols]).astype(BF)

    both = nn(perm_t[...], gp[:, QC:XC]).astype(BF)
    gk_ref[...] = both[:, :HD]
    gv_ref[...] = both[:, HD:]

    @pl.loop(1, NCHIP)
    def _(k):
        m = lax.rem(chip + k, NCHIP)
        weight_copy(m, m).wait()

    total = wr[0].astype(F32)
    for m in range(1, NCHIP):
        total = total + wr[m].astype(F32)
    wg_ref[...] = total

    for way in (0, 1):
        for half in (0, 1):
            rs_copy(way, 3, half).wait_recv()
    total = part[0].astype(F32) + rs_recv[0, 3].astype(F32) + rs_recv[1, 3].astype(F32)
    lo_ref[...] = total.astype(BF)

    for way in (0, 1):
        for step in range(4):
            for half in (0, 1):
                if half in ag_halves(way, step):
                    ag_copy(way, step, half).wait_send()
                if half in ag_halves(way, 3 - step):
                    rs_copy(way, step, half).wait_send()
    for rel in range(NT):
        sibling_copy(rel).wait_send()


def shards(query_rows, key_rows, value_rows, out_grad, w_out, lengths, target):
    vmem = pl.BlockSpec(memory_space=pltpu.VMEM)
    hbm = pl.BlockSpec(memory_space=pl.ANY)
    dma = pltpu.SemaphoreType.DMA
    outs = (
        jax.ShapeDtypeStruct((CAP, MC), BF),
        jax.ShapeDtypeStruct((PACK, QC), BF),
        jax.ShapeDtypeStruct((PACK, HD), BF),
        jax.ShapeDtypeStruct((PACK, HD), BF),
        jax.ShapeDtypeStruct((QC, 128), F32),
    )
    scratch = [
        pltpu.VMEM((PACK, XC), BF),
        pltpu.VMEM((PACK, XC), BF),
        pltpu.VMEM((NT, CAP, MC), BF),
        pltpu.VMEM((QC, NT * MC), BF),
        pltpu.VMEM((PACK, PACK), BF),
        pltpu.VMEM((PACK, PACK), BF),
        pltpu.VMEM((CAP, PACK), BF),
        pltpu.VMEM((PACK, CAP), BF),
        pltpu.VMEM((PACK, 128), F32),
        pltpu.VMEM((8, PACK), F32),
        pltpu.VMEM((PACK, 128), F32),
        pltpu.VMEM((8, PACK), F32),
        pltpu.VMEM((TILE, QC), F32),
        pltpu.VMEM((PACK // TILE, TILE, QC), F32),
        pltpu.VMEM((PACK, QC), BF),
        pltpu.VMEM((PACK, QC), BF),
        pltpu.VMEM((CAP, QC), BF),
        pltpu.VMEM((QC, CAP), BF),
        pltpu.VMEM((NT, CAP, MC), BF),
        pltpu.VMEM((2, 4, CAP, MC), BF),
        pltpu.VMEM((CAP, QC), F32),
        pltpu.VMEM((2, NCHIP, QC, 128), BF),
        pltpu.VMEM((NCHIP, QC, 128), BF),
        pltpu.VMEM((NCHIP, QC, 128), BF),
        pltpu.VMEM((PACK, QC), BF),
        pltpu.VMEM((PACK, QC), BF),
        pltpu.VMEM((PACK, XC), BF),
        dma((5,)),
        dma((2, 4, 2)),
        dma((2, 4, 2)),
        dma((2, 4, 2)),
        dma((2, 4, 2)),
        dma((NDP,)),
        dma((NDP,)),
        dma((NDP,)),
        dma((NDP,)),
        dma((NT,)),
        dma((NT,)),
        dma((NCHIP,)),
        dma((NCHIP,)),
    ]
    return pl.pallas_call(
        kernel,
        out_shape=outs,
        in_specs=[hbm, hbm, hbm, hbm, hbm, vmem, vmem],
        out_specs=(vmem,) * 5,
        scratch_shapes=scratch,
        compiler_params=pltpu.CompilerParams(
            collective_id=0, has_side_effects=True, vmem_limit_bytes=60 * 2**20
        ),
    )(query_rows, key_rows, value_rows, out_grad, w_out, lengths, target)


def solution(mesh):
    return jax.shard_map(
        shards,
        mesh=mesh,
        in_specs=(
            P("dp", "tensor"),
            P("dp", "tensor"),
            P("dp", "tensor"),
            P("dp", "tensor"),
            P("tensor", None),
            P(),
            P(),
        ),
        out_specs=(
            P("dp", "tensor"),
            P("dp", "tensor"),
            P("dp", "tensor"),
            P("dp", "tensor"),
            P("tensor", "dp"),
        ),
        check_vma=False,
    )
```

```python
import jax
import jax.numpy as jnp
from jax import lax
from jax.experimental import pallas as pl
from jax.experimental.pallas import tpu as pltpu
from jax.sharding import PartitionSpec as P

HD = 128
GROUP = 4
QC = GROUP * HD
XC = QC + 2 * HD
SLOT = 32
NDP = 32
NCHIP = NDP // 2
NT = 8
PACK = NDP * SLOT
CAP = 512
MC = 512
TILE = 128
HALF = CAP // 2
SCALE = HD**-0.5
OFF = 4096.0
BF = jnp.bfloat16
F32 = jnp.float32
MESH = pl.DeviceIdType.MESH


def nn(a, b):
    return lax.dot_general(a, b, (((1,), (0,)), ((), ())), preferred_element_type=F32)


def nt(a, b):
    return lax.dot_general(a, b, (((1,), (1,)), ((), ())), preferred_element_type=F32)


def tn(a, b):
    return lax.dot_general(a, b, (((0,), (0,)), ((), ())), preferred_element_type=F32)


def iota(shape, dim):
    return lax.broadcasted_iota(jnp.int32, shape, dim)


def one_hot(mask):
    return jnp.where(mask, 1.0, 0.0).astype(BF)


def remote(src, dst, send, recv, where):
    return pltpu.make_async_remote_copy(
        src_ref=src, dst_ref=dst, send_sem=send, recv_sem=recv, device_id=where, device_id_type=MESH
    )


def slot_index(member, starts, sizes):
    high = jnp.floor(starts * (1.0 / SLOT))
    low = starts - high * SLOT
    slot_col = (iota((PACK, 1), 0) % SLOT).astype(F32)
    slot_row = (iota((1, PACK), 1) % SLOT).astype(F32)
    start_col = jnp.sum(jnp.where(member, starts[0:1], 0.0), axis=1, keepdims=True)
    size_col = jnp.sum(jnp.where(member, sizes[0:1], 0.0), axis=1, keepdims=True)
    picks = one_hot(member)
    start_row = nt(high.astype(BF), picks)[0:1] * SLOT + nt(low.astype(BF), picks)[0:1]
    size_row = nt(sizes.astype(BF), picks)[0:1]
    col = jnp.where(slot_col < size_col, start_col + slot_col, OFF)
    row = jnp.where(slot_row < size_row, start_row + slot_row, OFF)
    return col, row


def kernel(
    q_in, k_in, v_in, og_in, w_in, len_ref, tgt_ref,
    lo_out, gq_out, gk_out, gv_out, wg_out,
    home, pieces, og, w, perm, perm_t, sel, sel_t, home_col, home_row, bal_col, bal_row, bias, probs,
    ctx_send, ctx_recv, bctx, bctx_t, part, rs_recv, dbal, wp, sx, wsum, wfar, wnear, vsum, vfar, vnear,
    d_send, d_recv, gp,
    lo, gq, gk, gv, wg,
    load_sem, ag_send, ag_recv, rs_send, rs_recv_sem, c_send, c_recv, d_ssem, d_rsem,
    x_send, x_recv, w_send, w_recv, store_sem,
):
    me = lax.axis_index("dp")
    z = lax.axis_index("tensor")
    core = lax.rem(me, 2)
    chip = lax.div(me, 2)
    right, left = {"tensor": lax.rem(z + 1, NT)}, {"tensor": lax.rem(z + NT - 1, NT)}
    toward = (right, left)
    sibling = {"dp": me + 1 - 2 * core}

    loads = [
        pltpu.make_async_copy(q_in, home.at[:, pl.ds(0, QC)], load_sem.at[0]),
        pltpu.make_async_copy(k_in, home.at[:, pl.ds(QC, HD)], load_sem.at[1]),
        pltpu.make_async_copy(v_in, home.at[:, pl.ds(QC + HD, HD)], load_sem.at[2]),
        pltpu.make_async_copy(og_in, og.at[0], load_sem.at[3]),
        pltpu.make_async_copy(w_in, w, load_sem.at[4]),
    ]
    for one in (loads[3], loads[0], loads[1], loads[2], loads[4]):
        one.start()

    barrier = pltpu.get_barrier_semaphore()
    pl.semaphore_signal(barrier, inc=1, device_id=right, device_id_type=MESH)
    pl.semaphore_signal(barrier, inc=1, device_id=left, device_id_type=MESH)

    @pl.loop(1, NDP)
    def _(k):
        pl.semaphore_signal(
            barrier, inc=1, device_id={"dp": lax.rem(me + k, NDP)}, device_id_type=MESH
        )

    pl.semaphore_wait(barrier, NDP + 1)

    halves = (pl.ds(0, HALF), pl.ds(HALF, HALF))

    def ag_copy(way, step, half):
        src = (NT - step) % NT if way == 0 else step
        dst = (NT - step - 1) % NT if way == 0 else step + 1
        return remote(
            og.at[src, halves[half]],
            og.at[dst, halves[half]],
            ag_send.at[way, step, half],
            ag_recv.at[way, step, half],
            toward[way],
        )

    def ag_halves(way, step):
        return (0, 1) if step < 3 else (way,)

    def ag_step(step, parts=(0, 1)):
        for half in parts:
            for way in (0, 1):
                if step > 0:
                    ag_copy(way, step - 1, half if way == 0 else 1 - half).wait_recv()
                order = half if way == 0 else 1 - half
                if order in ag_halves(way, step):
                    ag_copy(way, step, order).start()

    loads[3].wait()
    ag_step(0)

    lane = iota((NDP, NDP), 1)
    before = jnp.where(iota((NDP, NDP), 0) < lane, 1.0, 0.0).astype(BF)
    sizes = jnp.broadcast_to(len_ref[pl.ds(me, 1), :].astype(F32), (8, NDP))
    starts = nn(sizes.astype(BF), before)
    doc_of = lax.div(iota((PACK, NDP), 0), SLOT)
    col, row = slot_index(tgt_ref[pl.ds(me, 1), :] == doc_of, starts, sizes)
    home_col[...] = jnp.broadcast_to(col, (PACK, 128))
    home_row[...] = jnp.broadcast_to(row, (8, PACK))

    @pl.loop(0, PACK // TILE)
    def _(i):
        rows = pl.ds(pl.multiple_of(i * TILE, TILE), TILE)
        index = home_col[rows, 0:1]
        perm[rows, :] = one_hot(index == iota((TILE, PACK), 1).astype(F32))

    for one in loads[:3]:
        one.wait()

    @pl.loop(0, XC // 256)
    def _(i):
        cols = pl.ds(pl.multiple_of(i * 256, 256), 256)
        pieces[:, cols] = nn(perm[...], home[:, cols]).astype(BF)

    key_row = iota((TILE, QC), 0)
    query_row = iota((TILE, QC), 1) % TILE
    allowed = (lax.div(key_row, SLOT) == lax.div(query_row, SLOT)) & (key_row <= query_row)
    bias[...] = jnp.where(allowed, 0.0, -1e30)

    def heads(ref, rows):
        return jnp.concatenate([ref[rows, h * HD : (h + 1) * HD] for h in range(GROUP)], axis=0)

    def forward(i):
        rows = pl.ds(pl.multiple_of(i * TILE, TILE), TILE)
        scores = nt(pieces[rows, QC : QC + HD], heads(pieces, rows)) * SCALE + bias[...]
        weights = jnp.exp(scores - jnp.max(scores, axis=0, keepdims=True))
        weights = weights / jnp.sum(weights, axis=0, keepdims=True)
        probs[i] = weights
        context = tn(weights.astype(BF), pieces[rows, QC + HD : XC]).astype(BF)
        for h in range(GROUP):
            ctx_send[rows, h * HD : (h + 1) * HD] = context[h * TILE : (h + 1) * TILE]

    pl.loop(0, 4)(forward)
    ag_step(1, (0,))
    pl.loop(4, 8)(forward)

    def piece(d):
        return pl.ds(pl.multiple_of(d * SLOT, SLOT), SLOT)

    def exchange_start(source, dest, send, recv):
        @pl.loop(1, NDP)
        def _(k):
            d = lax.rem(me + k, NDP)
            remote(
                source.at[piece(d)], dest.at[piece(me)], send.at[d], recv.at[me], {"dp": d}
            ).start()

        dest[piece(me), :] = source[piece(me), :]

    def exchange_wait(source, dest, send, recv):
        @pl.loop(1, NDP)
        def _(k):
            d = lax.rem(me + k, NDP)
            remote(
                source.at[piece(d)], dest.at[piece(d)], send.at[d], recv.at[d], {"dp": d}
            ).wait()

    exchange_start(ctx_send, ctx_recv, c_send, c_recv)
    ag_step(1, (1,))

    sent_here = jnp.where(tgt_ref[...] == me, len_ref[...], 0).astype(F32).astype(BF)
    sizes = nt(jnp.ones((8, NDP), BF), sent_here)
    starts = nn(sizes.astype(BF), before)
    col, row = slot_index(iota((PACK, NDP), 1) == doc_of, starts, sizes)
    bal_col[...] = jnp.broadcast_to(col, (PACK, 128))
    bal_row[...] = jnp.broadcast_to(row, (8, PACK))

    @pl.loop(0, CAP // TILE)
    def _(i):
        rows = pl.ds(pl.multiple_of(i * TILE, TILE), TILE)
        here = (iota((TILE, PACK), 0) + i * TILE).astype(F32)
        sel[rows, :] = one_hot(bal_row[0:1, :] == here)

    loads[4].wait()

    def model_cols(rel):
        owner = lax.rem(z + rel, NT)
        return owner, pl.ds(pl.multiple_of(owner * MC, MC), MC)

    def add_dbalanced(rel, first=False):
        _, cols = model_cols(rel)
        term = nt(og[rel], w[:, cols])
        dbal[...] = term if first else dbal[...] + term

    add_dbalanced(0, True)
    add_dbalanced(1)
    add_dbalanced(7)

    @pl.loop(0, PACK // TILE)
    def _(i):
        rows = pl.ds(pl.multiple_of(i * TILE, TILE), TILE)
        here = (iota((TILE, PACK), 0) + i * TILE).astype(F32)
        perm_t[rows, :] = one_hot(home_row[0:1, :] == here)
        index = bal_col[rows, 0:1]
        sel_t[rows, :] = one_hot(index == iota((TILE, CAP), 1).astype(F32))

    ag_step(2)
    add_dbalanced(2)
    add_dbalanced(6)

    exchange_wait(ctx_send, ctx_recv, c_send, c_recv)
    balanced = nn(sel[...], ctx_recv[...]).astype(BF)
    bctx[...] = balanced
    bctx_t[...] = balanced.T

    def project(rel):
        _, cols = model_cols(rel)
        part[rel] = nn(bctx[...], w[:, cols]).astype(BF)

    def rs_copy(way, step, half):
        rel = 4 - step if way == 0 else 4 + step
        return remote(
            part.at[rel, halves[half]],
            rs_recv.at[way, step, halves[half]],
            rs_send.at[way, step, half],
            rs_recv_sem.at[way, step, half],
            toward[way],
        )

    def rs_step(step):
        for half in (1, 0):
            for way in (0, 1):
                order = half if way == 0 else 1 - half
                rel = 4 - step if way == 0 else 4 + step
                if order in ag_halves(way, 3 if step == 1 else 0):
                    rs_copy(way, step - 1, order).wait_recv()
                    rows = halves[order]
                    total = part[rel, rows].astype(F32) + rs_recv[way, step - 1, rows].astype(F32)
                    part[rel, rows] = total.astype(BF)
                    rs_copy(way, step, order).start()

    def weight_block(rel):
        owner, _ = model_cols(rel)
        grad = nn(bctx_t[...], og[rel]).astype(BF)
        for j in range(4):
            wp[lax.rem(core + j, 2), 2 * owner + j // 2] = grad[:, j * 128 : (j + 1) * 128]

    def sibling_copy(rel):
        owner, _ = model_cols(rel)
        both = pl.ds(2 * owner, 2)
        return remote(wp.at[1, both], sx.at[both], x_send.at[rel], x_recv.at[rel], sibling)

    def weight_sum(rel):
        owner, _ = model_cols(rel)
        sibling_copy(rel).wait_recv()
        for j in range(2):
            m = 2 * owner + j
            total = (wp[0, m].astype(F32) + sx[m].astype(F32)).astype(BF)
            wsum[0, lax.rem(m, 4) * 4 + lax.div(m, 4)] = total[:HALF]
            wsum[1, m] = total[HALF:]

    col_of, row_of = lax.rem(chip, 4), lax.div(chip, 4)

    def chip_ring(stage, part_of):
        along_x = stage == part_of
        at = col_of if along_x else row_of

        def spot(k):
            there = lax.rem(at + k, 4)
            number = row_of * 4 + there if along_x else there * 4 + col_of
            return {"dp": 2 * number + core}

        def piece_of(k, high):
            bundle = lax.rem(at + k, 4)
            if stage == 0:
                return (part_of, pl.ds(4 * bundle + 2 * high, 2))
            return (part_of, bundle, pl.ds(128 * high, 128))

        def near_of(way, high):
            return (part_of, way, pl.ds(2 * high, 2) if stage == 0 else pl.ds(128 * high, 128))

        source, far, near = (wsum, wfar, wnear) if stage == 0 else (vsum, vfar, vnear)

        def copy(number):
            way = number % 2
            if number < 2:
                src, dst = piece_of(2, way), (part_of, way)
            else:
                high = 1 - way if number < 4 else way
                src, dst = piece_of(1 if way == 0 else 3, high), near_of(way, high)
            return remote(
                source.at[src],
                far.at[dst] if number < 2 else near.at[dst],
                w_send.at[stage, part_of, number],
                w_recv.at[stage, part_of, number],
                spot(1 if way == 0 else 3),
            )

        def begin():
            for number in range(4):
                copy(number).start()

        def pass_on():
            for way in (0, 1):
                copy(way).wait_recv()
                where = piece_of(1 if way == 0 else 3, way)
                total = source[where].astype(F32) + far[part_of, way].astype(F32)
                source[where] = total.astype(BF)
                copy(4 + way).start()

        def finish():
            for number in range(2, 6):
                copy(number).wait_recv()
            own = (part_of, pl.ds(4 * at, 4)) if stage == 0 else (part_of, at)
            total = source[own].astype(F32) + near[part_of, 0].astype(F32)
            return total + near[part_of, 1].astype(F32)

        def drain():
            for number in range(6):
                copy(number).wait_send()

        return begin, pass_on, finish, drain

    rings = [[chip_ring(stage, part_of) for part_of in (0, 1)] for stage in (0, 1)]

    project(4)
    rs_copy(0, 0, 0).start()
    rs_copy(1, 0, 1).start()
    for rel in (0, 1, 7):
        weight_block(rel)
        sibling_copy(rel).start()
    ag_step(3)
    project(3)
    project(5)
    add_dbalanced(3)
    add_dbalanced(5)
    for rel in (2, 6):
        weight_block(rel)
        sibling_copy(rel).start()
    for rel in (0, 1, 7):
        weight_sum(rel)
    ag_copy(0, 3, 0).wait_recv()
    ag_copy(1, 3, 1).wait_recv()
    rs_copy(0, 1, 1).start()
    rs_copy(1, 1, 0).start()
    add_dbalanced(4)
    d_send[...] = nn(sel_t[...], dbal[...].astype(BF)).astype(BF)
    exchange_start(d_send, d_recv, d_ssem, d_rsem)
    rs_step(1)
    for rel in (3, 5, 4):
        weight_block(rel)
        sibling_copy(rel).start()
    project(2)
    project(6)
    for rel in (2, 6, 3, 5, 4):
        weight_sum(rel)
    for ring in rings[0]:
        ring[0]()
    rs_step(2)
    project(1)
    project(7)
    project(0)
    for ring in rings[0]:
        ring[1]()
    rs_step(3)
    exchange_wait(d_send, d_recv, d_ssem, d_rsem)

    def backward(i):
        rows = pl.ds(pl.multiple_of(i * TILE, TILE), TILE)
        weights = probs[i]
        half = weights.astype(BF)
        dcontext = heads(d_recv, rows)
        dweights = nt(pieces[rows, QC + HD : XC], dcontext)
        delta = jnp.sum(half.astype(F32) * dweights, axis=0, keepdims=True)
        dscores = (weights * (dweights - delta) * SCALE).astype(BF)
        dq = tn(dscores, pieces[rows, QC : QC + HD]).astype(BF)
        for h in range(GROUP):
            gp[rows, h * HD : (h + 1) * HD] = dq[h * TILE : (h + 1) * TILE]
        gp[rows, QC : QC + HD] = nn(dscores, heads(pieces, rows)).astype(BF)
        gp[rows, QC + HD : XC] = nn(half, dcontext).astype(BF)

    pl.loop(0, 4)(backward)
    for half, ring in enumerate(rings[0]):
        vsum[half] = ring[2]().astype(BF)
    for ring in rings[1]:
        ring[0]()
    pl.loop(4, 8)(backward)
    for ring in rings[1]:
        ring[1]()

    @pl.loop(0, QC // 256)
    def _(i):
        cols = pl.ds(pl.multiple_of(i * 256, 256), 256)
        gq[:, cols] = nn(perm_t[...], gp[:, cols]).astype(BF)

    both = nn(perm_t[...], gp[:, QC:XC]).astype(BF)
    gk[...] = both[:, :HD]
    gv[...] = both[:, HD:]
    stores = [
        pltpu.make_async_copy(src, dst, store_sem.at[i])
        for i, (src, dst) in enumerate(
            ((gq, gq_out), (gk, gk_out), (gv, gv_out), (wg, wg_out), (lo, lo_out))
        )
    ]
    for one in stores[:3]:
        one.start()

    for half, ring in enumerate(rings[1]):
        wg[half * HALF : (half + 1) * HALF, :] = ring[2]()
    stores[3].start()

    for way in (0, 1):
        for half in (0, 1):
            rs_copy(way, 3, half).wait_recv()
    total = part[0].astype(F32) + rs_recv[0, 3].astype(F32) + rs_recv[1, 3].astype(F32)
    lo[...] = total.astype(BF)
    stores[4].start()

    for way in (0, 1):
        for step in range(4):
            for half in (0, 1):
                if half in ag_halves(way, step):
                    ag_copy(way, step, half).wait_send()
                if half in ag_halves(way, 3 - step):
                    rs_copy(way, step, half).wait_send()
    for rel in range(NT):
        sibling_copy(rel).wait_send()
    for ring in rings[0] + rings[1]:
        ring[3]()
    for one in stores:
        one.wait()


def hand_over(*refs):
    sources, dests, stage, sems = refs[:5], refs[5:10], refs[10:15], refs[15]
    loads = [pltpu.make_async_copy(sources[i], stage[i], sems.at[0, i]) for i in range(5)]
    stores = [pltpu.make_async_copy(stage[i], dests[i], sems.at[1, i]) for i in range(5)]
    for one in loads:
        one.start()
    for load, store in zip(loads, stores):
        load.wait()
        store.start()
    for one in stores:
        one.wait()


def shards(query_rows, key_rows, value_rows, out_grad, w_out, lengths, target):
    vmem = pl.BlockSpec(memory_space=pltpu.VMEM)
    hbm = pl.BlockSpec(memory_space=pl.ANY)
    dma = pltpu.SemaphoreType.DMA
    outs = (
        jax.ShapeDtypeStruct((CAP, MC), BF),
        jax.ShapeDtypeStruct((PACK, QC), BF),
        jax.ShapeDtypeStruct((PACK, HD), BF),
        jax.ShapeDtypeStruct((PACK, HD), BF),
        jax.ShapeDtypeStruct((QC, 128), F32),
    )
    scratch = [
        pltpu.VMEM((PACK, XC), BF),
        pltpu.VMEM((PACK, XC), BF),
        pltpu.VMEM((NT, CAP, MC), BF),
        pltpu.VMEM((QC, NT * MC), BF),
        pltpu.VMEM((PACK, PACK), BF),
        pltpu.VMEM((PACK, PACK), BF),
        pltpu.VMEM((CAP, PACK), BF),
        pltpu.VMEM((PACK, CAP), BF),
        pltpu.VMEM((PACK, 128), F32),
        pltpu.VMEM((8, PACK), F32),
        pltpu.VMEM((PACK, 128), F32),
        pltpu.VMEM((8, PACK), F32),
        pltpu.VMEM((TILE, QC), F32),
        pltpu.VMEM((PACK // TILE, TILE, QC), F32),
        pltpu.VMEM((PACK, QC), BF),
        pltpu.VMEM((PACK, QC), BF),
        pltpu.VMEM((CAP, QC), BF),
        pltpu.VMEM((QC, CAP), BF),
        pltpu.VMEM((NT, CAP, MC), BF),
        pltpu.VMEM((2, 4, CAP, MC), BF),
        pltpu.VMEM((CAP, QC), F32),
        pltpu.VMEM((2, NCHIP, QC, 128), BF),
        pltpu.VMEM((NCHIP, QC, 128), BF),
        pltpu.VMEM((2, NCHIP, HALF, 128), BF),
        pltpu.VMEM((2, 2, 2, HALF, 128), BF),
        pltpu.VMEM((2, 2, 4, HALF, 128), BF),
        pltpu.VMEM((2, 4, HALF, 128), BF),
        pltpu.VMEM((2, 2, 128, 128), BF),
        pltpu.VMEM((2, 2, HALF, 128), BF),
        pltpu.VMEM((PACK, QC), BF),
        pltpu.VMEM((PACK, QC), BF),
        pltpu.VMEM((PACK, XC), BF),
        pltpu.VMEM((CAP, MC), BF),
        pltpu.VMEM((PACK, QC), BF),
        pltpu.VMEM((PACK, HD), BF),
        pltpu.VMEM((PACK, HD), BF),
        pltpu.VMEM((QC, 128), F32),
        dma((5,)),
        dma((2, 4, 2)),
        dma((2, 4, 2)),
        dma((2, 4, 2)),
        dma((2, 4, 2)),
        dma((NDP,)),
        dma((NDP,)),
        dma((NDP,)),
        dma((NDP,)),
        dma((NT,)),
        dma((NT,)),
        dma((2, 2, 6)),
        dma((2, 2, 6)),
        dma((5,)),
    ]
    results = pl.pallas_call(
        kernel,
        out_shape=outs,
        in_specs=[hbm, hbm, hbm, hbm, hbm, vmem, vmem],
        out_specs=(hbm,) * 5,
        scratch_shapes=scratch,
        compiler_params=pltpu.CompilerParams(
            collective_id=0, has_side_effects=True, vmem_limit_bytes=60 * 2**20
        ),
    )(query_rows, key_rows, value_rows, out_grad, w_out, lengths, target)
    return pl.pallas_call(
        hand_over,
        out_shape=outs,
        in_specs=[hbm] * 5,
        out_specs=(hbm,) * 5,
        scratch_shapes=[pltpu.VMEM(o.shape, o.dtype) for o in outs] + [dma((2, 5))],
    )(*results)


def solution(mesh):
    return jax.shard_map(
        shards,
        mesh=mesh,
        in_specs=(
            P("dp", "tensor"),
            P("dp", "tensor"),
            P("dp", "tensor"),
            P("dp", "tensor"),
            P("tensor", None),
            P(),
            P(),
        ),
        out_specs=(
            P("dp", "tensor"),
            P("dp", "tensor"),
            P("dp", "tensor"),
            P("dp", "tensor"),
            P("tensor", "dp"),
        ),
        check_vma=False,
    )
```

```python
import jax
import jax.numpy as jnp
from jax import lax
from jax.experimental import pallas as pl
from jax.experimental.pallas import tpu as pltpu
from jax.sharding import PartitionSpec as P

HD = 128
GROUP = 4
QC = GROUP * HD
XC = QC + 2 * HD
SLOT = 32
NDP = 32
NCHIP = NDP // 2
NT = 8
PACK = NDP * SLOT
CAP = 512
MC = 512
TILE = 128
HALF = CAP // 2
SCALE = HD**-0.5
OFF = 4096.0
BF = jnp.bfloat16
F32 = jnp.float32
MESH = pl.DeviceIdType.MESH


def nn(a, b):
    return lax.dot_general(a, b, (((1,), (0,)), ((), ())), preferred_element_type=F32)


def nt(a, b):
    return lax.dot_general(a, b, (((1,), (1,)), ((), ())), preferred_element_type=F32)


def tn(a, b):
    return lax.dot_general(a, b, (((0,), (0,)), ((), ())), preferred_element_type=F32)


def iota(shape, dim):
    return lax.broadcasted_iota(jnp.int32, shape, dim)


def one_hot(mask):
    return jnp.where(mask, 1.0, 0.0).astype(BF)


def remote(src, dst, send, recv, where):
    return pltpu.make_async_remote_copy(
        src_ref=src, dst_ref=dst, send_sem=send, recv_sem=recv, device_id=where, device_id_type=MESH
    )


def slot_index(member, starts, sizes):
    high = jnp.floor(starts * (1.0 / SLOT))
    low = starts - high * SLOT
    slot_col = (iota((PACK, 1), 0) % SLOT).astype(F32)
    slot_row = (iota((1, PACK), 1) % SLOT).astype(F32)
    start_col = jnp.sum(jnp.where(member, starts[0:1], 0.0), axis=1, keepdims=True)
    size_col = jnp.sum(jnp.where(member, sizes[0:1], 0.0), axis=1, keepdims=True)
    picks = one_hot(member)
    start_row = nt(high.astype(BF), picks)[0:1] * SLOT + nt(low.astype(BF), picks)[0:1]
    size_row = nt(sizes.astype(BF), picks)[0:1]
    col = jnp.where(slot_col < size_col, start_col + slot_col, OFF)
    row = jnp.where(slot_row < size_row, start_row + slot_row, OFF)
    return col, row


def kernel(
    q_in, k_in, v_in, og_in, w_in, len_ref, tgt_ref,
    lo_out, gq_out, gk_out, gv_out, wg_out,
    home, pieces, og, w, perm, perm_t, sel, sel_t, home_col, home_row, bal_col, bal_row, bias, probs,
    ctx_send, ctx_recv, bctx, bctx_t, p_end, p_mid, c_out, r_in, r_out, r_own, wx, dbal, wp, sx, wsum, wfar, wnear, vsum, vfar, vnear,
    d_send, d_recv, gp,
    lo, gq, gk, gv, wg,
    load_sem, ag_send, ag_recv, rs_send, rs_recv, wz_send, wz_recv, wa_send, wa_recv, c_send, c_recv, d_ssem, d_rsem,
    x_send, x_recv, w_send, w_recv, store_sem,
):
    me = lax.axis_index("dp")
    z = lax.axis_index("tensor")
    core = lax.rem(me, 2)
    chip = lax.div(me, 2)
    right, left = {"tensor": lax.rem(z + 1, NT)}, {"tensor": lax.rem(z + NT - 1, NT)}
    toward = (right, left)
    sibling = {"dp": me + 1 - 2 * core}
    col_of, row_of = lax.rem(chip, 4), lax.div(chip, 4)

    sign = 1 - 2 * lax.rem(z, 2)

    def plane(k):
        return lax.rem(z + sign * k + 2 * NT, NT)

    loads = [
        pltpu.make_async_copy(q_in, home.at[:, pl.ds(0, QC)], load_sem.at[0]),
        pltpu.make_async_copy(k_in, home.at[:, pl.ds(QC, HD)], load_sem.at[1]),
        pltpu.make_async_copy(v_in, home.at[:, pl.ds(QC + HD, HD)], load_sem.at[2]),
        pltpu.make_async_copy(og_in, og.at[0], load_sem.at[3]),
        pltpu.make_async_copy(w_in, w, load_sem.at[4]),
    ]
    for one in (loads[3], loads[0], loads[1], loads[2], loads[4]):
        one.start()

    barrier = pltpu.get_barrier_semaphore()
    pl.semaphore_signal(barrier, inc=1, device_id=right, device_id_type=MESH)
    pl.semaphore_signal(barrier, inc=1, device_id=left, device_id_type=MESH)
    for k in (2, NT - 2):
        pl.semaphore_signal(
            barrier, inc=1, device_id={"tensor": lax.rem(z + k, NT)}, device_id_type=MESH
        )

    @pl.loop(1, NDP)
    def _(k):
        pl.semaphore_signal(
            barrier, inc=1, device_id={"dp": lax.rem(me + k, NDP)}, device_id_type=MESH
        )

    pl.semaphore_wait(barrier, NDP + 3)

    halves = (pl.ds(0, HALF), pl.ds(HALF, HALF))

    def ag_copy(way, step, half):
        src = (NT - step) % NT if way == 0 else step
        dst = (NT - step - 1) % NT if way == 0 else step + 1
        return remote(
            og.at[src, halves[half]],
            og.at[dst, halves[half]],
            ag_send.at[way, step, half],
            ag_recv.at[way, step, half],
            toward[way],
        )

    def ag_halves(way, step):
        return (0, 1) if step < 3 else (way,)

    def ag_step(step, parts=(0, 1)):
        for half in parts:
            for way in (0, 1):
                if step > 0:
                    ag_copy(way, step - 1, half if way == 0 else 1 - half).wait_recv()
                order = half if way == 0 else 1 - half
                if order in ag_halves(way, step):
                    ag_copy(way, step, order).start()

    def wz_copy(i, j):
        a, b = (col_of, row_of) if i == 0 else (row_of, col_of)
        rows = pl.ds(pl.multiple_of(256 * core + 64 * b + 16 * a, 16), 16)
        cols = pl.ds(pl.multiple_of(plane(-1 - j if i == 0 else 2 + j) * MC, MC), MC)
        return remote(
            w_in.at[rows, cols],
            wx.at[i, j, rows],
            wz_send.at[i, j],
            wz_recv.at[i, j],
            {"tensor": plane(-1 if i == 0 else 2)},
        )

    def chip_at(along_x, k):
        there = lax.rem((col_of if along_x else row_of) + k, 4)
        number = row_of * 4 + there if along_x else there * 4 + col_of
        return {"dp": 2 * number + core}

    def wa_copy(i, stage, number):
        a, b = (col_of, row_of) if i == 0 else (row_of, col_of)
        along_x = (i == 0) == (stage == 0)
        way = number % 2
        step = 0 if number < 2 else 3 if way == 0 else 1
        if stage == 0:
            start = 256 * core + 64 * b + 16 * lax.rem(a + step, 4)
            rows = pl.ds(pl.multiple_of(start, 16), 16)
        else:
            rows = pl.ds(pl.multiple_of(256 * core + 64 * lax.rem(b + step, 4), 64), 64)
        blocks = pl.ds(0, 4) if number < 2 else pl.ds(2 * way, 2)
        ref = wx.at[i, blocks, rows]
        return remote(
            ref,
            ref,
            wa_send.at[i, stage, number],
            wa_recv.at[i, stage, number],
            chip_at(along_x, 1 if way == 0 else 3),
        )

    def wx_sibling(i):
        ref = wx.at[i, :, pl.ds(pl.multiple_of(256 * core, 256), 256)]
        return remote(ref, ref, wa_send.at[i, 2, 0], wa_recv.at[i, 2, 0], sibling)

    def wx_step(step):
        for i in (0, 1):
            if step == 0:
                for j in range(4):
                    wz_copy(i, j).wait_recv()
            elif step < 5:
                for way in (0, 1):
                    wa_copy(i, (step - 1) // 2, way + 2 * ((step - 1) % 2)).wait_recv()
            else:
                wx_sibling(i).wait_recv()
            if step < 4:
                for way in (0, 1):
                    wa_copy(i, step // 2, way + 2 * (step % 2)).start()
            elif step == 4:
                wx_sibling(i).start()

    for j in range(4):
        for i in (0, 1):
            wz_copy(i, j).start()
    loads[3].wait()
    ag_step(0)

    lane = iota((NDP, NDP), 1)
    before = jnp.where(iota((NDP, NDP), 0) < lane, 1.0, 0.0).astype(BF)
    sizes = jnp.broadcast_to(len_ref[pl.ds(me, 1), :].astype(F32), (8, NDP))
    starts = nn(sizes.astype(BF), before)
    doc_of = lax.div(iota((PACK, NDP), 0), SLOT)
    col, row = slot_index(tgt_ref[pl.ds(me, 1), :] == doc_of, starts, sizes)
    home_col[...] = jnp.broadcast_to(col, (PACK, 128))
    home_row[...] = jnp.broadcast_to(row, (8, PACK))

    @pl.loop(0, PACK // TILE)
    def _(i):
        rows = pl.ds(pl.multiple_of(i * TILE, TILE), TILE)
        index = home_col[rows, 0:1]
        perm[rows, :] = one_hot(index == iota((TILE, PACK), 1).astype(F32))

    for one in loads[:3]:
        one.wait()

    @pl.loop(0, XC // 256)
    def _(i):
        cols = pl.ds(pl.multiple_of(i * 256, 256), 256)
        pieces[:, cols] = nn(perm[...], home[:, cols]).astype(BF)

    wx_step(0)

    key_row = iota((TILE, QC), 0)
    query_row = iota((TILE, QC), 1) % TILE
    allowed = (lax.div(key_row, SLOT) == lax.div(query_row, SLOT)) & (key_row <= query_row)
    bias[...] = jnp.where(allowed, 0.0, -1e30)

    def heads(ref, rows):
        return jnp.concatenate([ref[rows, h * HD : (h + 1) * HD] for h in range(GROUP)], axis=0)

    def forward(i):
        rows = pl.ds(pl.multiple_of(i * TILE, TILE), TILE)
        scores = nt(pieces[rows, QC : QC + HD], heads(pieces, rows)) * SCALE + bias[...]
        weights = jnp.exp(scores - jnp.max(scores, axis=0, keepdims=True))
        weights = weights / jnp.sum(weights, axis=0, keepdims=True)
        probs[i] = weights
        context = tn(weights.astype(BF), pieces[rows, QC + HD : XC]).astype(BF)
        for h in range(GROUP):
            ctx_send[rows, h * HD : (h + 1) * HD] = context[h * TILE : (h + 1) * TILE]

    def piece(d):
        return pl.ds(pl.multiple_of(d * SLOT, SLOT), SLOT)

    def forward_and_send(i):
        tile = lax.rem(lax.div(me, 4) + i, PACK // TILE)
        forward(tile)
        for j in range(4):
            d = 4 * tile + j

            @pl.when(d != me)
            def _():
                remote(
                    ctx_send.at[piece(d)], ctx_recv.at[piece(me)], c_send.at[d], c_recv.at[me], {"dp": d}
                ).start()

    pl.loop(0, 4)(forward_and_send)
    wx_step(1)
    ag_step(1, (0,))
    pl.loop(4, 8)(forward_and_send)
    ctx_recv[piece(me), :] = ctx_send[piece(me), :]

    def exchange_start(source, dest, send, recv):
        @pl.loop(1, NDP)
        def _(k):
            d = lax.rem(me + k, NDP)
            remote(
                source.at[piece(d)], dest.at[piece(me)], send.at[d], recv.at[me], {"dp": d}
            ).start()

        dest[piece(me), :] = source[piece(me), :]

    def exchange_wait(source, dest, send, recv):
        @pl.loop(1, NDP)
        def _(k):
            d = lax.rem(me + k, NDP)
            remote(
                source.at[piece(d)], dest.at[piece(d)], send.at[d], recv.at[d], {"dp": d}
            ).wait()

    ag_step(1, (1,))

    sent_here = jnp.where(tgt_ref[...] == me, len_ref[...], 0).astype(F32).astype(BF)
    sizes = nt(jnp.ones((8, NDP), BF), sent_here)
    starts = nn(sizes.astype(BF), before)
    col, row = slot_index(iota((PACK, NDP), 1) == doc_of, starts, sizes)
    bal_col[...] = jnp.broadcast_to(col, (PACK, 128))
    bal_row[...] = jnp.broadcast_to(row, (8, PACK))

    @pl.loop(0, CAP // TILE)
    def _(i):
        rows = pl.ds(pl.multiple_of(i * TILE, TILE), TILE)
        here = (iota((TILE, PACK), 0) + i * TILE).astype(F32)
        sel[rows, :] = one_hot(bal_row[0:1, :] == here)

    loads[4].wait()

    def model_cols(rel):
        owner = lax.rem(z + rel, NT)
        return owner, pl.ds(pl.multiple_of(owner * MC, MC), MC)

    def add_dbalanced(rel, first=False):
        _, cols = model_cols(rel)
        term = nt(og[rel], w[:, cols])
        dbal[...] = term if first else dbal[...] + term

    add_dbalanced(0, True)
    add_dbalanced(1)
    add_dbalanced(7)

    @pl.loop(0, PACK // TILE)
    def _(i):
        rows = pl.ds(pl.multiple_of(i * TILE, TILE), TILE)
        here = (iota((TILE, PACK), 0) + i * TILE).astype(F32)
        perm_t[rows, :] = one_hot(home_row[0:1, :] == here)
        index = bal_col[rows, 0:1]
        sel_t[rows, :] = one_hot(index == iota((TILE, CAP), 1).astype(F32))

    wx_step(2)
    ag_step(2)
    wx_step(3)
    add_dbalanced(2)
    add_dbalanced(6)

    exchange_wait(ctx_send, ctx_recv, c_send, c_recv)
    balanced = nn(sel[...], ctx_recv[...]).astype(BF)
    bctx[...] = balanced
    bctx_t[...] = balanced.T

    quarter = lax.rem(z, 4)
    end = lax.rem(lax.div(quarter + 1, 2), 2)
    end_rows = pl.ds(pl.multiple_of(end * HALF, HALF), HALF)
    mid_rows = pl.ds(pl.multiple_of((1 - end) * HALF, HALF), HALF)
    partner, other = {"tensor": plane(1)}, {"tensor": plane(-1)}

    def plane_cols(k):
        return pl.ds(pl.multiple_of(plane(k) * MC, MC), MC)

    def rs_copy(number):
        src, dst, where = (
            (bctx.at[end_rows], c_out.at[0], other),
            (bctx.at[mid_rows], c_out.at[1], {"tensor": plane(2)}),
            (p_end.at[1], r_in.at[0], partner),
            (p_end.at[2], r_in.at[1], partner),
            (p_end.at[3], r_in.at[2], partner),
            (p_mid.at[2], r_out.at[0], other),
            (p_mid.at[3], r_out.at[1], other),
            (p_mid.at[1], r_own, partner),
        )[number]
        return remote(src, dst, rs_send.at[number], rs_recv.at[number], where)

    def project_mid():
        for slot, k in enumerate((0, 1, -1, -2)):
            p_mid[slot] = nn(bctx[mid_rows, :], w[:, plane_cols(k)]).astype(BF)

    def project_end(k):
        total = nn(bctx[end_rows, :], w[:, plane_cols(k)])
        total = total + nn(c_out[0], wx[0, k]) + nn(c_out[1], wx[1, k])
        p_end[k] = total.astype(BF)

    def pass_on(slot, ref, number):
        p_mid[slot] = (p_mid[slot].astype(F32) + ref[...].astype(F32)).astype(BF)
        rs_copy(number).start()

    def weight_block(rel):
        owner, _ = model_cols(rel)
        grad = nn(bctx_t[...], og[rel]).astype(BF)
        for j in range(4):
            wp[lax.rem(core + j, 2), 2 * owner + j // 2] = grad[:, j * 128 : (j + 1) * 128]

    def sibling_copy(rel):
        owner, _ = model_cols(rel)
        both = pl.ds(2 * owner, 2)
        return remote(wp.at[1, both], sx.at[both], x_send.at[rel], x_recv.at[rel], sibling)

    def weight_sum(rel):
        owner, _ = model_cols(rel)
        sibling_copy(rel).wait_recv()
        for j in range(2):
            m = 2 * owner + j
            total = (wp[0, m].astype(F32) + sx[m].astype(F32)).astype(BF)
            wsum[0, lax.rem(m, 4) * 4 + lax.div(m, 4)] = total[:HALF]
            wsum[1, m] = total[HALF:]

    def chip_ring(stage, part_of):
        along_x = stage == part_of
        at = col_of if along_x else row_of

        def piece_of(k, high):
            bundle = lax.rem(at + k, 4)
            if stage == 0:
                return (part_of, pl.ds(4 * bundle + 2 * high, 2))
            return (part_of, bundle, pl.ds(128 * high, 128))

        def near_of(way, high):
            return (part_of, way, pl.ds(2 * high, 2) if stage == 0 else pl.ds(128 * high, 128))

        source, far, near = (wsum, wfar, wnear) if stage == 0 else (vsum, vfar, vnear)

        def copy(number):
            way = number % 2
            if number < 2:
                src, dst = piece_of(2, way), (part_of, way)
            else:
                high = 1 - way if number < 4 else way
                src, dst = piece_of(1 if way == 0 else 3, high), near_of(way, high)
            return remote(
                source.at[src],
                far.at[dst] if number < 2 else near.at[dst],
                w_send.at[stage, part_of, number],
                w_recv.at[stage, part_of, number],
                chip_at(along_x, 1 if way == 0 else 3),
            )

        def begin():
            for number in range(4):
                copy(number).start()

        def pass_on():
            for way in (0, 1):
                copy(way).wait_recv()
                where = piece_of(1 if way == 0 else 3, way)
                total = source[where].astype(F32) + far[part_of, way].astype(F32)
                source[where] = total.astype(BF)
                copy(4 + way).start()

        def finish():
            for number in range(2, 6):
                copy(number).wait_recv()
            own = (part_of, pl.ds(4 * at, 4)) if stage == 0 else (part_of, at)
            total = source[own].astype(F32) + near[part_of, 0].astype(F32)
            return total + near[part_of, 1].astype(F32)

        def drain():
            for number in range(6):
                copy(number).wait_send()

        return begin, pass_on, finish, drain

    rings = [[chip_ring(stage, part_of) for part_of in (0, 1)] for stage in (0, 1)]

    wx_step(4)
    project_mid()
    for rel in (0, 1, 7):
        weight_block(rel)
        sibling_copy(rel).start()
    ag_step(3)
    rs_copy(1).start()
    rs_copy(0).start()
    add_dbalanced(3)
    add_dbalanced(5)
    for rel in (2, 6):
        weight_block(rel)
        sibling_copy(rel).start()
    for rel in (0, 1, 7):
        weight_sum(rel)
    ag_copy(0, 3, 0).wait_recv()
    ag_copy(1, 3, 1).wait_recv()
    add_dbalanced(4)
    d_send[...] = nn(sel_t[...], dbal[...].astype(BF)).astype(BF)
    exchange_start(d_send, d_recv, d_ssem, d_rsem)
    wx_step(5)
    rs_copy(0).wait_recv()
    rs_copy(1).wait_recv()
    for k in (3, 2, 1):
        project_end(k)
        rs_copy(1 + k).start()
    for rel in (3, 5, 4):
        weight_block(rel)
        sibling_copy(rel).start()
    project_end(0)
    for rel in (2, 6, 3, 5, 4):
        weight_sum(rel)
    for ring in rings[0]:
        ring[0]()
    rs_copy(4).wait_recv()
    pass_on(3, r_in.at[2], 6)
    for ring in rings[0]:
        ring[1]()
    rs_copy(3).wait_recv()
    pass_on(2, r_in.at[1], 5)
    rs_copy(6).wait_recv()
    pass_on(1, r_out.at[1], 7)

    def backward(i):
        tile = lax.rem(lax.div(me, 4) + 8 - i, PACK // TILE)
        for j in range(4):
            d = 4 * tile + j

            @pl.when(d != me)
            def _():
                remote(
                    d_send.at[piece(d)], d_recv.at[piece(d)], d_ssem.at[d], d_rsem.at[d], {"dp": d}
                ).wait()

        rows = pl.ds(pl.multiple_of(tile * TILE, TILE), TILE)
        weights = probs[tile]
        half = weights.astype(BF)
        dcontext = heads(d_recv, rows)
        dweights = nt(pieces[rows, QC + HD : XC], dcontext)
        delta = jnp.sum(half.astype(F32) * dweights, axis=0, keepdims=True)
        dscores = (weights * (dweights - delta) * SCALE).astype(BF)
        dq = tn(dscores, pieces[rows, QC : QC + HD]).astype(BF)
        for h in range(GROUP):
            gp[rows, h * HD : (h + 1) * HD] = dq[h * TILE : (h + 1) * TILE]
        gp[rows, QC : QC + HD] = nn(dscores, heads(pieces, rows)).astype(BF)
        gp[rows, QC + HD : XC] = nn(half, dcontext).astype(BF)

    pl.loop(0, 4)(backward)
    for half, ring in enumerate(rings[0]):
        vsum[half] = ring[2]().astype(BF)
    for ring in rings[1]:
        ring[0]()
    pl.loop(4, 8)(backward)
    for ring in rings[1]:
        ring[1]()

    @pl.loop(0, QC // 256)
    def _(i):
        cols = pl.ds(pl.multiple_of(i * 256, 256), 256)
        gq[:, cols] = nn(perm_t[...], gp[:, cols]).astype(BF)

    both = nn(perm_t[...], gp[:, QC:XC]).astype(BF)
    gk[...] = both[:, :HD]
    gv[...] = both[:, HD:]
    stores = [
        pltpu.make_async_copy(src, dst, store_sem.at[i])
        for i, (src, dst) in enumerate(
            ((gq, gq_out), (gk, gk_out), (gv, gv_out), (wg, wg_out), (lo, lo_out))
        )
    ]
    for one in stores[:3]:
        one.start()

    for half, ring in enumerate(rings[1]):
        wg[half * HALF : (half + 1) * HALF, :] = ring[2]()
    stores[3].start()

    for number in (2, 5):
        rs_copy(number).wait_recv()
    total = p_mid[0].astype(F32) + r_in[0].astype(F32) + r_out[0].astype(F32)
    lo[mid_rows, :] = total.astype(BF)
    rs_copy(7).wait_recv()
    total = p_end[0].astype(F32) + r_own[...].astype(F32)
    lo[end_rows, :] = total.astype(BF)
    stores[4].start()

    for way in (0, 1):
        for step in range(4):
            for half in (0, 1):
                if half in ag_halves(way, step):
                    ag_copy(way, step, half).wait_send()
    for number in range(8):
        rs_copy(number).wait_send()
    for i in (0, 1):
        for j in range(4):
            wz_copy(i, j).wait_send()
            wa_copy(i, 0, j).wait_send()
            wa_copy(i, 1, j).wait_send()
        wx_sibling(i).wait_send()
    for rel in range(NT):
        sibling_copy(rel).wait_send()
    for ring in rings[0] + rings[1]:
        ring[3]()
    for one in stores:
        one.wait()


def hand_over(*refs):
    sources, dests, stage, sems = refs[:5], refs[5:10], refs[10:15], refs[15]
    loads = [pltpu.make_async_copy(sources[i], stage[i], sems.at[0, i]) for i in range(5)]
    stores = [pltpu.make_async_copy(stage[i], dests[i], sems.at[1, i]) for i in range(5)]
    for one in loads:
        one.start()
    for load, store in zip(loads, stores):
        load.wait()
        store.start()
    for one in stores:
        one.wait()


def shards(query_rows, key_rows, value_rows, out_grad, w_out, lengths, target):
    vmem = pl.BlockSpec(memory_space=pltpu.VMEM)
    hbm = pl.BlockSpec(memory_space=pl.ANY)
    dma = pltpu.SemaphoreType.DMA
    outs = (
        jax.ShapeDtypeStruct((CAP, MC), BF),
        jax.ShapeDtypeStruct((PACK, QC), BF),
        jax.ShapeDtypeStruct((PACK, HD), BF),
        jax.ShapeDtypeStruct((PACK, HD), BF),
        jax.ShapeDtypeStruct((QC, 128), F32),
    )
    scratch = [
        pltpu.VMEM((PACK, XC), BF),
        pltpu.VMEM((PACK, XC), BF),
        pltpu.VMEM((NT, CAP, MC), BF),
        pltpu.VMEM((QC, NT * MC), BF),
        pltpu.VMEM((PACK, PACK), BF),
        pltpu.VMEM((PACK, PACK), BF),
        pltpu.VMEM((CAP, PACK), BF),
        pltpu.VMEM((PACK, CAP), BF),
        pltpu.VMEM((PACK, 128), F32),
        pltpu.VMEM((8, PACK), F32),
        pltpu.VMEM((PACK, 128), F32),
        pltpu.VMEM((8, PACK), F32),
        pltpu.VMEM((TILE, QC), F32),
        pltpu.VMEM((PACK // TILE, TILE, QC), F32),
        pltpu.VMEM((PACK, QC), BF),
        pltpu.VMEM((PACK, QC), BF),
        pltpu.VMEM((CAP, QC), BF),
        pltpu.VMEM((QC, CAP), BF),
        pltpu.VMEM((4, HALF, MC), BF),
        pltpu.VMEM((4, HALF, MC), BF),
        pltpu.VMEM((2, HALF, QC), BF),
        pltpu.VMEM((3, HALF, MC), BF),
        pltpu.VMEM((2, HALF, MC), BF),
        pltpu.VMEM((HALF, MC), BF),
        pltpu.VMEM((2, 4, QC, MC), BF),
        pltpu.VMEM((CAP, QC), F32),
        pltpu.VMEM((2, NCHIP, QC, 128), BF),
        pltpu.VMEM((NCHIP, QC, 128), BF),
        pltpu.VMEM((2, NCHIP, HALF, 128), BF),
        pltpu.VMEM((2, 2, 2, HALF, 128), BF),
        pltpu.VMEM((2, 2, 4, HALF, 128), BF),
        pltpu.VMEM((2, 4, HALF, 128), BF),
        pltpu.VMEM((2, 2, 128, 128), BF),
        pltpu.VMEM((2, 2, HALF, 128), BF),
        pltpu.VMEM((PACK, QC), BF),
        pltpu.VMEM((PACK, QC), BF),
        pltpu.VMEM((PACK, XC), BF),
        pltpu.VMEM((CAP, MC), BF),
        pltpu.VMEM((PACK, QC), BF),
        pltpu.VMEM((PACK, HD), BF),
        pltpu.VMEM((PACK, HD), BF),
        pltpu.VMEM((QC, 128), F32),
        dma((5,)),
        dma((2, 4, 2)),
        dma((2, 4, 2)),
        dma((8,)),
        dma((8,)),
        dma((2, 4)),
        dma((2, 4)),
        dma((2, 3, 4)),
        dma((2, 3, 4)),
        dma((NDP,)),
        dma((NDP,)),
        dma((NDP,)),
        dma((NDP,)),
        dma((NT,)),
        dma((NT,)),
        dma((2, 2, 6)),
        dma((2, 2, 6)),
        dma((5,)),
    ]
    results = pl.pallas_call(
        kernel,
        out_shape=outs,
        in_specs=[hbm, hbm, hbm, hbm, hbm, vmem, vmem],
        out_specs=(hbm,) * 5,
        scratch_shapes=scratch,
        compiler_params=pltpu.CompilerParams(
            collective_id=0, has_side_effects=True, vmem_limit_bytes=60 * 2**20
        ),
    )(query_rows, key_rows, value_rows, out_grad, w_out, lengths, target)
    return pl.pallas_call(
        hand_over,
        out_shape=outs,
        in_specs=[hbm] * 5,
        out_specs=(hbm,) * 5,
        scratch_shapes=[pltpu.VMEM(o.shape, o.dtype) for o in outs] + [dma((2, 5))],
    )(*results)


def solution(mesh):
    return jax.shard_map(
        shards,
        mesh=mesh,
        in_specs=(
            P("dp", "tensor"),
            P("dp", "tensor"),
            P("dp", "tensor"),
            P("dp", "tensor"),
            P("tensor", None),
            P(),
            P(),
        ),
        out_specs=(
            P("dp", "tensor"),
            P("dp", "tensor"),
            P("dp", "tensor"),
            P("dp", "tensor"),
            P("tensor", "dp"),
        ),
        check_vma=False,
    )
```

```python
import jax
import jax.numpy as jnp
from jax import lax
from jax.experimental import pallas as pl
from jax.experimental.pallas import tpu as pltpu
from jax.sharding import PartitionSpec as P

HD = 128
GROUP = 4
QC = GROUP * HD
XC = QC + 2 * HD
SLOT = 32
NDP = 32
NCHIP = NDP // 2
NT = 8
PACK = NDP * SLOT
CAP = 512
MC = 512
TILE = 128
HALF = CAP // 2
SCALE = HD**-0.5
OFF = 4096.0
BF = jnp.bfloat16
F32 = jnp.float32
MESH = pl.DeviceIdType.MESH


def nn(a, b):
    return lax.dot_general(a, b, (((1,), (0,)), ((), ())), preferred_element_type=F32)


def nt(a, b):
    return lax.dot_general(a, b, (((1,), (1,)), ((), ())), preferred_element_type=F32)


def tn(a, b):
    return lax.dot_general(a, b, (((0,), (0,)), ((), ())), preferred_element_type=F32)


def iota(shape, dim):
    return lax.broadcasted_iota(jnp.int32, shape, dim)


def one_hot(mask):
    return jnp.where(mask, 1.0, 0.0).astype(BF)


def remote(src, dst, send, recv, where):
    return pltpu.make_async_remote_copy(
        src_ref=src, dst_ref=dst, send_sem=send, recv_sem=recv, device_id=where, device_id_type=MESH
    )


def slot_index(member, starts, sizes):
    high = jnp.floor(starts * (1.0 / SLOT))
    low = starts - high * SLOT
    slot_col = (iota((PACK, 1), 0) % SLOT).astype(F32)
    slot_row = (iota((1, PACK), 1) % SLOT).astype(F32)
    start_col = jnp.sum(jnp.where(member, starts[0:1], 0.0), axis=1, keepdims=True)
    size_col = jnp.sum(jnp.where(member, sizes[0:1], 0.0), axis=1, keepdims=True)
    picks = one_hot(member)
    start_row = nt(high.astype(BF), picks)[0:1] * SLOT + nt(low.astype(BF), picks)[0:1]
    size_row = nt(sizes.astype(BF), picks)[0:1]
    col = jnp.where(slot_col < size_col, start_col + slot_col, OFF)
    row = jnp.where(slot_row < size_row, start_row + slot_row, OFF)
    return col, row


def kernel(
    q_in, k_in, v_in, og_in, w_in, len_ref, tgt_ref,
    lo_out, gq_out, gk_out, gv_out, wg_out,
    home, pieces, og, w, perm, perm_t, sel, sel_t, home_col, home_row, bal_col, bal_row, bias, probs,
    ctx_send, ctx_recv, bctx, bctx_t, p_end, p_mid, c_out, r_in, r_out, r_own, wx, dbal, wp, sx, wsum, wfar, wnear, vsum, vfar, vnear,
    d_send, d_recv, gp,
    lo, gq, gk, gv, wg,
    load_sem, ag_send, ag_recv, rs_send, rs_recv, wz_send, wz_recv, wa_send, wa_recv, c_send, c_recv, d_ssem, d_rsem,
    x_send, x_recv, w_send, w_recv, store_sem,
):
    me = lax.axis_index("dp")
    z = lax.axis_index("tensor")
    core = lax.rem(me, 2)
    chip = lax.div(me, 2)
    right, left = {"tensor": lax.rem(z + 1, NT)}, {"tensor": lax.rem(z + NT - 1, NT)}
    toward = (right, left)
    sibling = {"dp": me + 1 - 2 * core}
    col_of, row_of = lax.rem(chip, 4), lax.div(chip, 4)

    sign = 1 - 2 * lax.rem(z, 2)

    def plane(k):
        return lax.rem(z + sign * k + 2 * NT, NT)

    loads = [
        pltpu.make_async_copy(q_in, home.at[:, pl.ds(0, QC)], load_sem.at[0]),
        pltpu.make_async_copy(k_in, home.at[:, pl.ds(QC, HD)], load_sem.at[1]),
        pltpu.make_async_copy(v_in, home.at[:, pl.ds(QC + HD, HD)], load_sem.at[2]),
        pltpu.make_async_copy(og_in, og.at[0], load_sem.at[3]),
        pltpu.make_async_copy(w_in, w, load_sem.at[4]),
    ]
    for one in (loads[3], loads[0], loads[1], loads[2], loads[4]):
        one.start()

    barrier = pltpu.get_barrier_semaphore()
    pl.semaphore_signal(barrier, inc=1, device_id=right, device_id_type=MESH)
    pl.semaphore_signal(barrier, inc=1, device_id=left, device_id_type=MESH)
    for k in (2, NT - 2):
        pl.semaphore_signal(
            barrier, inc=1, device_id={"tensor": lax.rem(z + k, NT)}, device_id_type=MESH
        )

    @pl.loop(1, NDP)
    def _(k):
        pl.semaphore_signal(
            barrier, inc=1, device_id={"dp": lax.rem(me + k, NDP)}, device_id_type=MESH
        )

    pl.semaphore_wait(barrier, NDP + 3)

    halves = (pl.ds(0, HALF), pl.ds(HALF, HALF))

    def ag_copy(way, step, half):
        src = (NT - step) % NT if way == 0 else step
        dst = (NT - step - 1) % NT if way == 0 else step + 1
        return remote(
            og.at[src, halves[half]],
            og.at[dst, halves[half]],
            ag_send.at[way, step, half],
            ag_recv.at[way, step, half],
            toward[way],
        )

    def ag_halves(way, step):
        return (0, 1) if step < 3 else (way,)

    def ag_step(step, parts=(0, 1)):
        for half in parts:
            for way in (0, 1):
                if step > 0:
                    ag_copy(way, step - 1, half if way == 0 else 1 - half).wait_recv()
                order = half if way == 0 else 1 - half
                if order in ag_halves(way, step):
                    ag_copy(way, step, order).start()

    def wz_copy(i, j):
        a, b = (col_of, row_of) if i == 0 else (row_of, col_of)
        rows = pl.ds(pl.multiple_of(256 * core + 64 * b + 16 * a, 16), 16)
        cols = pl.ds(pl.multiple_of(plane(-1 - j if i == 0 else 2 + j) * MC, MC), MC)
        return remote(
            w_in.at[rows, cols],
            wx.at[i, j, rows],
            wz_send.at[i, j],
            wz_recv.at[i, j],
            {"tensor": plane(-1 if i == 0 else 2)},
        )

    def chip_at(along_x, k):
        there = lax.rem((col_of if along_x else row_of) + k, 4)
        number = row_of * 4 + there if along_x else there * 4 + col_of
        return {"dp": 2 * number + core}

    def wa_copy(i, stage, number):
        a, b = (col_of, row_of) if i == 0 else (row_of, col_of)
        along_x = (i == 0) == (stage == 0)
        way = number % 2
        step = 0 if number < 2 else 3 if way == 0 else 1
        if stage == 0:
            start = 256 * core + 64 * b + 16 * lax.rem(a + step, 4)
            rows = pl.ds(pl.multiple_of(start, 16), 16)
        else:
            rows = pl.ds(pl.multiple_of(256 * core + 64 * lax.rem(b + step, 4), 64), 64)
        blocks = pl.ds(0, 4) if number < 2 else pl.ds(2 * way, 2)
        ref = wx.at[i, blocks, rows]
        return remote(
            ref,
            ref,
            wa_send.at[i, stage, number],
            wa_recv.at[i, stage, number],
            chip_at(along_x, 1 if way == 0 else 3),
        )

    def wx_sibling(i):
        ref = wx.at[i, :, pl.ds(pl.multiple_of(256 * core, 256), 256)]
        return remote(ref, ref, wa_send.at[i, 2, 0], wa_recv.at[i, 2, 0], sibling)

    def wx_step(step):
        for i in (0, 1):
            if step == 0:
                for j in range(4):
                    wz_copy(i, j).wait_recv()
            elif step < 5:
                for way in (0, 1):
                    wa_copy(i, (step - 1) // 2, way + 2 * ((step - 1) % 2)).wait_recv()
            else:
                wx_sibling(i).wait_recv()
            if step < 4:
                for way in (0, 1):
                    wa_copy(i, step // 2, way + 2 * (step % 2)).start()
            elif step == 4:
                wx_sibling(i).start()

    for j in range(4):
        for i in (0, 1):
            wz_copy(i, j).start()
    loads[3].wait()
    ag_step(0)

    lane = iota((NDP, NDP), 1)
    before = jnp.where(iota((NDP, NDP), 0) < lane, 1.0, 0.0).astype(BF)
    sizes = jnp.broadcast_to(len_ref[pl.ds(me, 1), :].astype(F32), (8, NDP))
    starts = nn(sizes.astype(BF), before)
    doc_of = lax.div(iota((PACK, NDP), 0), SLOT)
    col, row = slot_index(tgt_ref[pl.ds(me, 1), :] == doc_of, starts, sizes)
    home_col[...] = jnp.broadcast_to(col, (PACK, 128))
    home_row[...] = jnp.broadcast_to(row, (8, PACK))

    @pl.loop(0, PACK // TILE)
    def _(i):
        rows = pl.ds(pl.multiple_of(i * TILE, TILE), TILE)
        index = home_col[rows, 0:1]
        perm[rows, :] = one_hot(index == iota((TILE, PACK), 1).astype(F32))

    for one in loads[:3]:
        one.wait()

    @pl.loop(0, XC // 256)
    def _(i):
        cols = pl.ds(pl.multiple_of(i * 256, 256), 256)
        pieces[:, cols] = nn(perm[...], home[:, cols]).astype(BF)

    wx_step(0)

    key_row = iota((TILE, QC), 0)
    query_row = iota((TILE, QC), 1) % TILE
    allowed = (lax.div(key_row, SLOT) == lax.div(query_row, SLOT)) & (key_row <= query_row)
    bias[...] = jnp.where(allowed, 0.0, -1e30)

    def heads(ref, rows):
        return jnp.concatenate([ref[rows, h * HD : (h + 1) * HD] for h in range(GROUP)], axis=0)

    def forward(i):
        rows = pl.ds(pl.multiple_of(i * TILE, TILE), TILE)
        scores = nt(pieces[rows, QC : QC + HD], heads(pieces, rows)) * SCALE + bias[...]
        weights = jnp.exp(scores - jnp.max(scores, axis=0, keepdims=True))
        weights = weights / jnp.sum(weights, axis=0, keepdims=True)
        probs[i] = weights
        context = tn(weights.astype(BF), pieces[rows, QC + HD : XC]).astype(BF)
        for h in range(GROUP):
            ctx_send[rows, h * HD : (h + 1) * HD] = context[h * TILE : (h + 1) * TILE]

    def piece(d):
        return pl.ds(pl.multiple_of(d * SLOT, SLOT), SLOT)

    def forward_and_send(i):
        tile = lax.rem(lax.div(me, 4) + i, PACK // TILE)
        forward(tile)
        for j in range(4):
            d = 4 * tile + j

            @pl.when(d != me)
            def _():
                remote(
                    ctx_send.at[piece(d)], ctx_recv.at[piece(me)], c_send.at[d], c_recv.at[me], {"dp": d}
                ).start()

    pl.loop(0, 4)(forward_and_send)
    wx_step(1)
    ag_step(1, (0,))
    pl.loop(4, 8)(forward_and_send)
    ctx_recv[piece(me), :] = ctx_send[piece(me), :]

    def exchange_start(source, dest, send, recv):
        @pl.loop(1, NDP)
        def _(k):
            d = lax.rem(me + k, NDP)
            remote(
                source.at[piece(d)], dest.at[piece(me)], send.at[d], recv.at[me], {"dp": d}
            ).start()

        dest[piece(me), :] = source[piece(me), :]

    def exchange_wait(source, dest, send, recv):
        @pl.loop(1, NDP)
        def _(k):
            d = lax.rem(me + k, NDP)
            remote(
                source.at[piece(d)], dest.at[piece(d)], send.at[d], recv.at[d], {"dp": d}
            ).wait()

    ag_step(1, (1,))

    sent_here = jnp.where(tgt_ref[...] == me, len_ref[...], 0).astype(F32).astype(BF)
    sizes = nt(jnp.ones((8, NDP), BF), sent_here)
    starts = nn(sizes.astype(BF), before)
    col, row = slot_index(iota((PACK, NDP), 1) == doc_of, starts, sizes)
    bal_col[...] = jnp.broadcast_to(col, (PACK, 128))
    bal_row[...] = jnp.broadcast_to(row, (8, PACK))

    @pl.loop(0, CAP // TILE)
    def _(i):
        rows = pl.ds(pl.multiple_of(i * TILE, TILE), TILE)
        here = (iota((TILE, PACK), 0) + i * TILE).astype(F32)
        sel[rows, :] = one_hot(bal_row[0:1, :] == here)

    loads[4].wait()

    def model_cols(rel):
        owner = lax.rem(z + rel, NT)
        return owner, pl.ds(pl.multiple_of(owner * MC, MC), MC)

    def add_dbalanced(rel, first=False):
        _, cols = model_cols(rel)
        term = nt(og[rel], w[:, cols])
        dbal[...] = term if first else dbal[...] + term

    add_dbalanced(0, True)
    add_dbalanced(1)
    add_dbalanced(7)

    @pl.loop(0, PACK // TILE)
    def _(i):
        rows = pl.ds(pl.multiple_of(i * TILE, TILE), TILE)
        here = (iota((TILE, PACK), 0) + i * TILE).astype(F32)
        perm_t[rows, :] = one_hot(home_row[0:1, :] == here)
        index = bal_col[rows, 0:1]
        sel_t[rows, :] = one_hot(index == iota((TILE, CAP), 1).astype(F32))

    wx_step(2)
    ag_step(2)
    wx_step(3)
    add_dbalanced(2)
    add_dbalanced(6)

    exchange_wait(ctx_send, ctx_recv, c_send, c_recv)
    balanced = nn(sel[...], ctx_recv[...]).astype(BF)
    bctx[...] = balanced
    bctx_t[...] = balanced.T

    quarter = lax.rem(z, 4)
    end = lax.rem(lax.div(quarter + 1, 2), 2)
    mid = 1 - end
    halves_of = (pl.ds(0, TILE), pl.ds(TILE, TILE))

    def rows_at(half, sub):
        return pl.ds(pl.multiple_of(half * HALF + sub * TILE, TILE), TILE)

    partner, other = {"tensor": plane(1)}, {"tensor": plane(-1)}

    def plane_cols(k):
        return pl.ds(pl.multiple_of(plane(k) * MC, MC), MC)

    def rs_copy(number, sub):
        rows = halves_of[sub]
        src, dst, where = (
            (bctx.at[rows_at(end, sub)], c_out.at[0, rows], other),
            (bctx.at[rows_at(mid, sub)], c_out.at[1, rows], {"tensor": plane(2)}),
            (p_end.at[1, rows], r_in.at[0, rows], partner),
            (p_end.at[2, rows], r_in.at[1, rows], partner),
            (p_end.at[3, rows], r_in.at[2, rows], partner),
            (p_mid.at[2, rows], r_out.at[0, rows], other),
            (p_mid.at[3, rows], r_out.at[1, rows], other),
            (p_mid.at[1, rows], r_own.at[rows], partner),
        )[number]
        return remote(src, dst, rs_send.at[number, sub], rs_recv.at[number, sub], where)

    def project_mid():
        rows = pl.ds(pl.multiple_of(mid * HALF, HALF), HALF)
        for slot, k in enumerate((0, 1, -1, -2)):
            p_mid[slot] = nn(bctx[rows, :], w[:, plane_cols(k)]).astype(BF)

    def project_end(k, sub):
        rows = halves_of[sub]
        total = nn(bctx[rows_at(end, sub), :], w[:, plane_cols(k)])
        total = total + nn(c_out[0, rows], wx[0, k]) + nn(c_out[1, rows], wx[1, k])
        p_end[k, rows] = total.astype(BF)

    def pass_on(slot, ref, number, arrival):
        for sub, rows in enumerate(halves_of):
            rs_copy(arrival, sub).wait_recv()
            total = p_mid[slot, rows].astype(F32) + ref[rows].astype(F32)
            p_mid[slot, rows] = total.astype(BF)
            rs_copy(number, sub).start()

    def weight_block(rel):
        owner, _ = model_cols(rel)
        grad = nn(bctx_t[...], og[rel]).astype(BF)
        for j in range(4):
            wp[lax.rem(core + j, 2), 2 * owner + j // 2] = grad[:, j * 128 : (j + 1) * 128]

    def sibling_copy(rel):
        owner, _ = model_cols(rel)
        both = pl.ds(2 * owner, 2)
        return remote(wp.at[1, both], sx.at[both], x_send.at[rel], x_recv.at[rel], sibling)

    def weight_sum(rel):
        owner, _ = model_cols(rel)
        sibling_copy(rel).wait_recv()
        for j in range(2):
            m = 2 * owner + j
            total = (wp[0, m].astype(F32) + sx[m].astype(F32)).astype(BF)
            wsum[0, lax.rem(m, 4) * 4 + lax.div(m, 4)] = total[:HALF]
            wsum[1, m] = total[HALF:]

    def chip_ring(stage, part_of):
        along_x = stage == part_of
        at = col_of if along_x else row_of

        def piece_of(k, high):
            bundle = lax.rem(at + k, 4)
            if stage == 0:
                return (part_of, pl.ds(4 * bundle + 2 * high, 2))
            return (part_of, bundle, pl.ds(128 * high, 128))

        def near_of(way, high):
            return (part_of, way, pl.ds(2 * high, 2) if stage == 0 else pl.ds(128 * high, 128))

        source, far, near = (wsum, wfar, wnear) if stage == 0 else (vsum, vfar, vnear)

        def copy(number):
            way = number % 2
            if number < 2:
                src, dst = piece_of(2, way), (part_of, way)
            else:
                high = 1 - way if number < 4 else way
                src, dst = piece_of(1 if way == 0 else 3, high), near_of(way, high)
            return remote(
                source.at[src],
                far.at[dst] if number < 2 else near.at[dst],
                w_send.at[stage, part_of, number],
                w_recv.at[stage, part_of, number],
                chip_at(along_x, 1 if way == 0 else 3),
            )

        def begin():
            for number in range(4):
                copy(number).start()

        def pass_on():
            for way in (0, 1):
                copy(way).wait_recv()
                where = piece_of(1 if way == 0 else 3, way)
                total = source[where].astype(F32) + far[part_of, way].astype(F32)
                source[where] = total.astype(BF)
                copy(4 + way).start()

        def finish():
            for number in range(2, 6):
                copy(number).wait_recv()
            own = (part_of, pl.ds(4 * at, 4)) if stage == 0 else (part_of, at)
            total = source[own].astype(F32) + near[part_of, 0].astype(F32)
            return total + near[part_of, 1].astype(F32)

        def drain():
            for number in range(6):
                copy(number).wait_send()

        return begin, pass_on, finish, drain

    rings = [[chip_ring(stage, part_of) for part_of in (0, 1)] for stage in (0, 1)]

    wx_step(4)
    project_mid()
    for rel in (0, 1, 7):
        weight_block(rel)
        sibling_copy(rel).start()
    ag_step(3)
    for sub in (0, 1):
        rs_copy(1, sub).start()
        rs_copy(0, sub).start()
    add_dbalanced(3)
    add_dbalanced(5)
    for rel in (2, 6, 3, 5):
        weight_block(rel)
        sibling_copy(rel).start()
    for rel in (0, 1, 7, 2, 6, 3, 5):
        weight_sum(rel)
    ag_copy(0, 3, 0).wait_recv()
    ag_copy(1, 3, 1).wait_recv()
    add_dbalanced(4)
    d_send[...] = nn(sel_t[...], dbal[...].astype(BF)).astype(BF)
    exchange_start(d_send, d_recv, d_ssem, d_rsem)
    weight_block(4)
    sibling_copy(4).start()
    wx_step(5)
    weight_sum(4)
    for ring in rings[0]:
        ring[0]()
    for sub in (0, 1):
        rs_copy(0, sub).wait_recv()
        rs_copy(1, sub).wait_recv()
        for k in (3, 2, 1):
            project_end(k, sub)
            rs_copy(1 + k, sub).start()
        project_end(0, sub)
    pass_on(3, r_in.at[2], 6, 4)
    for ring in rings[0]:
        ring[1]()
    pass_on(2, r_in.at[1], 5, 3)
    pass_on(1, r_out.at[1], 7, 6)

    def backward(i):
        tile = lax.rem(lax.div(me, 4) + 8 - i, PACK // TILE)
        for j in range(4):
            d = 4 * tile + j

            @pl.when(d != me)
            def _():
                remote(
                    d_send.at[piece(d)], d_recv.at[piece(d)], d_ssem.at[d], d_rsem.at[d], {"dp": d}
                ).wait()

        rows = pl.ds(pl.multiple_of(tile * TILE, TILE), TILE)
        weights = probs[tile]
        half = weights.astype(BF)
        dcontext = heads(d_recv, rows)
        dweights = nt(pieces[rows, QC + HD : XC], dcontext)
        delta = jnp.sum(half.astype(F32) * dweights, axis=0, keepdims=True)
        dscores = (weights * (dweights - delta) * SCALE).astype(BF)
        dq = tn(dscores, pieces[rows, QC : QC + HD]).astype(BF)
        for h in range(GROUP):
            gp[rows, h * HD : (h + 1) * HD] = dq[h * TILE : (h + 1) * TILE]
        gp[rows, QC : QC + HD] = nn(dscores, heads(pieces, rows)).astype(BF)
        gp[rows, QC + HD : XC] = nn(half, dcontext).astype(BF)

    pl.loop(0, 4)(backward)
    for half, ring in enumerate(rings[0]):
        vsum[half] = ring[2]().astype(BF)
    for ring in rings[1]:
        ring[0]()
    pl.loop(4, 8)(backward)
    for ring in rings[1]:
        ring[1]()

    @pl.loop(0, QC // 256)
    def _(i):
        cols = pl.ds(pl.multiple_of(i * 256, 256), 256)
        gq[:, cols] = nn(perm_t[...], gp[:, cols]).astype(BF)

    both = nn(perm_t[...], gp[:, QC:XC]).astype(BF)
    gk[...] = both[:, :HD]
    gv[...] = both[:, HD:]
    stores = [
        pltpu.make_async_copy(src, dst, store_sem.at[i])
        for i, (src, dst) in enumerate(
            ((gq, gq_out), (gk, gk_out), (gv, gv_out), (wg, wg_out), (lo, lo_out))
        )
    ]
    for one in stores[:3]:
        one.start()

    for half, ring in enumerate(rings[1]):
        wg[half * HALF : (half + 1) * HALF, :] = ring[2]()
    stores[3].start()

    for sub, rows in enumerate(halves_of):
        rs_copy(2, sub).wait_recv()
        rs_copy(5, sub).wait_recv()
        total = p_mid[0, rows].astype(F32) + r_in[0, rows].astype(F32)
        lo[rows_at(mid, sub), :] = (total + r_out[0, rows].astype(F32)).astype(BF)
    for sub, rows in enumerate(halves_of):
        rs_copy(7, sub).wait_recv()
        total = p_end[0, rows].astype(F32) + r_own[rows].astype(F32)
        lo[rows_at(end, sub), :] = total.astype(BF)
    stores[4].start()

    for way in (0, 1):
        for step in range(4):
            for half in (0, 1):
                if half in ag_halves(way, step):
                    ag_copy(way, step, half).wait_send()
    for number in range(8):
        for sub in (0, 1):
            rs_copy(number, sub).wait_send()
    for i in (0, 1):
        for j in range(4):
            wz_copy(i, j).wait_send()
            wa_copy(i, 0, j).wait_send()
            wa_copy(i, 1, j).wait_send()
        wx_sibling(i).wait_send()
    for rel in range(NT):
        sibling_copy(rel).wait_send()
    for ring in rings[0] + rings[1]:
        ring[3]()
    for one in stores:
        one.wait()


def hand_over(*refs):
    sources, dests, stage, sems = refs[:5], refs[5:10], refs[10:15], refs[15]
    loads = [pltpu.make_async_copy(sources[i], stage[i], sems.at[0, i]) for i in range(5)]
    stores = [pltpu.make_async_copy(stage[i], dests[i], sems.at[1, i]) for i in range(5)]
    for one in loads:
        one.start()
    for load, store in zip(loads, stores):
        load.wait()
        store.start()
    for one in stores:
        one.wait()


def shards(query_rows, key_rows, value_rows, out_grad, w_out, lengths, target):
    vmem = pl.BlockSpec(memory_space=pltpu.VMEM)
    hbm = pl.BlockSpec(memory_space=pl.ANY)
    dma = pltpu.SemaphoreType.DMA
    outs = (
        jax.ShapeDtypeStruct((CAP, MC), BF),
        jax.ShapeDtypeStruct((PACK, QC), BF),
        jax.ShapeDtypeStruct((PACK, HD), BF),
        jax.ShapeDtypeStruct((PACK, HD), BF),
        jax.ShapeDtypeStruct((QC, 128), F32),
    )
    scratch = [
        pltpu.VMEM((PACK, XC), BF),
        pltpu.VMEM((PACK, XC), BF),
        pltpu.VMEM((NT, CAP, MC), BF),
        pltpu.VMEM((QC, NT * MC), BF),
        pltpu.VMEM((PACK, PACK), BF),
        pltpu.VMEM((PACK, PACK), BF),
        pltpu.VMEM((CAP, PACK), BF),
        pltpu.VMEM((PACK, CAP), BF),
        pltpu.VMEM((PACK, 128), F32),
        pltpu.VMEM((8, PACK), F32),
        pltpu.VMEM((PACK, 128), F32),
        pltpu.VMEM((8, PACK), F32),
        pltpu.VMEM((TILE, QC), F32),
        pltpu.VMEM((PACK // TILE, TILE, QC), F32),
        pltpu.VMEM((PACK, QC), BF),
        pltpu.VMEM((PACK, QC), BF),
        pltpu.VMEM((CAP, QC), BF),
        pltpu.VMEM((QC, CAP), BF),
        pltpu.VMEM((4, HALF, MC), BF),
        pltpu.VMEM((4, HALF, MC), BF),
        pltpu.VMEM((2, HALF, QC), BF),
        pltpu.VMEM((3, HALF, MC), BF),
        pltpu.VMEM((2, HALF, MC), BF),
        pltpu.VMEM((HALF, MC), BF),
        pltpu.VMEM((2, 4, QC, MC), BF),
        pltpu.VMEM((CAP, QC), F32),
        pltpu.VMEM((2, NCHIP, QC, 128), BF),
        pltpu.VMEM((NCHIP, QC, 128), BF),
        pltpu.VMEM((2, NCHIP, HALF, 128), BF),
        pltpu.VMEM((2, 2, 2, HALF, 128), BF),
        pltpu.VMEM((2, 2, 4, HALF, 128), BF),
        pltpu.VMEM((2, 4, HALF, 128), BF),
        pltpu.VMEM((2, 2, 128, 128), BF),
        pltpu.VMEM((2, 2, HALF, 128), BF),
        pltpu.VMEM((PACK, QC), BF),
        pltpu.VMEM((PACK, QC), BF),
        pltpu.VMEM((PACK, XC), BF),
        pltpu.VMEM((CAP, MC), BF),
        pltpu.VMEM((PACK, QC), BF),
        pltpu.VMEM((PACK, HD), BF),
        pltpu.VMEM((PACK, HD), BF),
        pltpu.VMEM((QC, 128), F32),
        dma((5,)),
        dma((2, 4, 2)),
        dma((2, 4, 2)),
        dma((8, 2)),
        dma((8, 2)),
        dma((2, 4)),
        dma((2, 4)),
        dma((2, 3, 4)),
        dma((2, 3, 4)),
        dma((NDP,)),
        dma((NDP,)),
        dma((NDP,)),
        dma((NDP,)),
        dma((NT,)),
        dma((NT,)),
        dma((2, 2, 6)),
        dma((2, 2, 6)),
        dma((5,)),
    ]
    results = pl.pallas_call(
        kernel,
        out_shape=outs,
        in_specs=[hbm, hbm, hbm, hbm, hbm, vmem, vmem],
        out_specs=(hbm,) * 5,
        scratch_shapes=scratch,
        compiler_params=pltpu.CompilerParams(
            collective_id=0, has_side_effects=True, vmem_limit_bytes=60 * 2**20
        ),
    )(query_rows, key_rows, value_rows, out_grad, w_out, lengths, target)
    return pl.pallas_call(
        hand_over,
        out_shape=outs,
        in_specs=[hbm] * 5,
        out_specs=(hbm,) * 5,
        scratch_shapes=[pltpu.VMEM(o.shape, o.dtype) for o in outs] + [dma((2, 5))],
    )(*results)


def solution(mesh):
    return jax.shard_map(
        shards,
        mesh=mesh,
        in_specs=(
            P("dp", "tensor"),
            P("dp", "tensor"),
            P("dp", "tensor"),
            P("dp", "tensor"),
            P("tensor", None),
            P(),
            P(),
        ),
        out_specs=(
            P("dp", "tensor"),
            P("dp", "tensor"),
            P("dp", "tensor"),
            P("dp", "tensor"),
            P("tensor", "dp"),
        ),
        check_vma=False,
    )
```
